128 devices in a mesh: row: 32 (over z, y, core), col: 4 (over x).
Axes of the slice: x: 4, y: 4, z: 4, core: 2. Of those that a mesh axis runs over, the one named last changes fastest.
Arguments:
- design: float32 [32768, 4096], P('row', 'col')
- signs: int32 [32768], P('row'), may hold values from -1 to 1, as said below
- sample_rows: int32 [8192], P('row'), may hold values from 0 to 32767
Outputs:
- sketch: float32 [8192, 4096], P('row', 'col')
- gram: float32 [4096, 4096], P('row', 'col')
The draws below stay inside these ranges and needn't reach their ends.
Inputs may be any that keep to these rules, and one draw needn't show every extreme that they name: `signs`: every entry is -1 or 1.
All inputs are finite; a program needn't handle non-finite values.
Results may differ from the reference program's by a relative error of at most 0.0003.
Values sent between devices are 32-bit elements; how exact they have to be, the bound alone decides.
No kernel may reach another device: no remote copies, remote signals or barrier semaphores. Data moves between devices by JAX's collectives and lax.ppermute only.
A program may use at most 320 MiB of HBM per device.

```python
import jax
import jax.numpy as jnp
from jax import lax

NCOL = 4096
ROW_DEV = 1024
ROWS = 32768
SAMPLES = 8192
N_ROW = 32


def draw_design(key, part):
    key = jax.random.fold_in(key, 11)
    key_main, key_scale = jax.random.split(key, 2)
    base = jax.random.normal(key_main, (ROWS, NCOL), jnp.float32)
    scales = jnp.exp(jax.random.uniform(key_scale, (1, NCOL), jnp.float32, 0.0, 1.15))
    return base * scales / jnp.sqrt(jnp.float32(ROWS))


def draw_signs(key, part):
    key = jax.random.fold_in(key, 5)
    return (2 * jax.random.randint(key, (ROWS,), 0, 2) - 1).astype(jnp.int32)


def plant(result, stream_key, smallest, top_value):
    longest = result.shape.index(max(result.shape))
    spots = []
    for shift in (0, 1):
        where = [jax.random.randint(jax.random.fold_in(stream_key, axis), (), 0, length) for axis, length in enumerate(result.shape)]
        where[longest] = (where[longest] + shift) % result.shape[longest]
        spots.append(tuple(where))
    return result.at[spots[0]].set(smallest).at[spots[1]].set(top_value)


def setup_inputs(seed: int = 0) -> dict:
    streams_of = jax.random.split(jax.random.key(seed), 4)
    design = draw_design(jax.random.fold_in(streams_of[3], 71), 0)
    signs = draw_signs(jax.random.fold_in(streams_of[3], 71), 0)
    sample_rows = plant(jax.random.randint(streams_of[2], (SAMPLES,), 0, ROWS), jax.random.fold_in(streams_of[2], 1), 0, ROWS - 1).astype(jnp.int32)
    return {"design": design, "signs": signs, "sample_rows": sample_rows}


def hadamard(order):
    index = jnp.arange(order, dtype=jnp.int32)
    both = index[:, None] & index[None, :]
    count = jnp.zeros((order, order), jnp.int32)
    for bit in range(max(order.bit_length() - 1, 0)):
        count = count + (both >> bit & 1)
    return (1 - 2 * (count % 2)).astype(jnp.float32)

def reference(design, signs, sample_rows):
    bits = ROW_DEV.bit_length() - 1
    first = 2 ** (bits // 2)
    second = ROW_DEV // first
    table_first = hadamard(first)
    table_second = hadamard(second)
    table_outer = hadamard(N_ROW)
    block_cols = min(512, NCOL)
    blocks = NCOL // block_cols
    owner_block = (sample_rows // ROW_DEV).astype(jnp.int32)
    inner_row = (sample_rows % ROW_DEV).astype(jnp.int32)
    mixing = table_outer[owner_block]
    sign_float = signs.astype(jnp.float32)

    def one_block(number):
        piece = lax.dynamic_slice_in_dim(design, (number * block_cols).astype(jnp.int32), block_cols, 1)
        piece = (piece * sign_float[:, None]).reshape(N_ROW, first, second, block_cols)
        piece = jnp.einsum('ij,njbc->nibc', table_first, piece, precision=lax.Precision.HIGHEST)
        piece = jnp.einsum('kb,nibc->nikc', table_second, piece, precision=lax.Precision.HIGHEST)
        piece = piece.reshape(N_ROW, ROW_DEV, block_cols)[:, inner_row]
        return jnp.einsum('kn,nkc->kc', mixing, piece, precision=lax.Precision.HIGHEST)
    stacked = lax.map(one_block, jnp.arange(blocks, dtype=jnp.int32))
    sketch = jnp.transpose(stacked, (1, 0, 2)).reshape(SAMPLES, NCOL)
    sketch = sketch * (1.0 / jnp.sqrt(jnp.float32(SAMPLES)))
    gram = jnp.dot(sketch.T, sketch, precision=lax.Precision.HIGHEST, preferred_element_type=jnp.float32)
    return (sketch, gram)
```

```python
import functools

import jax
import jax.numpy as jnp
import numpy as np
from jax import lax
from jax.experimental import pallas as pl
from jax.experimental.pallas import tpu as pltpu
from jax.sharding import PartitionSpec as P

NZ = NY = 4
SIDE = 4
LANE = 128
VMEM = 56 * 2**20


def place(z, y, c):
    return (z % NZ) * 2 * NY + (y % NY) * 2 + c


FIRST = [[place(z, y, 0) for y in range(4)] for z in range(4)]
FIRST += [[place(z, y, 1) for z in range(4)] for y in range(4)]
SECOND = [[place(z, y, 0) for z in range(4)] for y in range(4)]
SECOND += [[place(z, y, 1) for y in range(4)] for z in range(4)]
SIBLING = [(i, i ^ 1) for i in range(32)]


def around(step):
    return [(i, (i + step) % SIDE) for i in range(SIDE)]


def hadamard(order):
    index = np.arange(order)
    both = index[:, None] & index[None, :]
    count = np.zeros((order, order), np.int64)
    for bit in range(order.bit_length() - 1):
        count += both >> bit & 1
    return 1 - 2 * (count % 2)


def split(value):
    high = value.astype(jnp.bfloat16)
    low = (value - high.astype(jnp.float32)).astype(jnp.bfloat16)
    return high, low


def butterfly(parts):
    half = len(parts) // 2
    if half == 0:
        return parts
    low, high = butterfly(parts[:half]), butterfly(parts[half:])
    return [a + b for a, b in zip(low, high)] + [a - b for a, b in zip(low, high)]


def local_kernel(which_ref, table_ref, signs_ref, design_ref, out_ref):
    parts = []
    size = table_ref.shape[0]
    for number in range(design_ref.shape[0] // size):
        rows = pl.ds(number * size, size)
        signed = design_ref[rows, :] * signs_ref[rows, :]
        high, low = split(signed)
        part = jnp.dot(table_ref[...], high, preferred_element_type=jnp.float32)
        part += jnp.dot(table_ref[...], low, preferred_element_type=jnp.float32)
        parts.append(part)
    for number, part in enumerate(butterfly(parts)):
        out_ref[0, pl.ds(number * size, size), :] = part


def local_transform(design, signs, table, which):
    rows, width = design.shape
    blocks = width // (2 * LANE)
    size = table.shape[0]
    return pl.pallas_call(
        local_kernel,
        grid_spec=pltpu.PrefetchScalarGridSpec(
            num_scalar_prefetch=1,
            grid=(blocks,),
            in_specs=[
                pl.BlockSpec((size, size), lambda j, w: (0, 0)),
                pl.BlockSpec((rows, 1), lambda j, w: (0, 0)),
                pl.BlockSpec((rows, LANE), lambda j, w: (0, 2 * j + w[0])),
            ],
            out_specs=pl.BlockSpec((1, rows, LANE), lambda j, w: (j, 0, 0)),
        ),
        out_shape=jax.ShapeDtypeStruct((blocks, rows, LANE), jnp.float32),
        compiler_params=pltpu.CompilerParams(vmem_limit_bytes=VMEM),
        cost_estimate=pl.CostEstimate(flops=2**30, bytes_accessed=2**22, transcendentals=0),
    )(which, table, signs, design)


def sample_kernel(scale, index_ref, own_ref, other_ref, out_ref, mixed_ref):
    rows = own_ref.shape[1]
    step = pl.program_id(0)

    @pl.when(step == 0)
    def _():
        chunk = 64

        @pl.loop(0, rows // chunk)
        def _(number):
            here = pl.ds(number * chunk, chunk)
            sums, differences = [], []
            for src in range(SIDE):
                own, other = own_ref[src, here, :] * scale, other_ref[src, here, :] * scale
                sums.append(own + other)
                differences.append(own - other)
            for core, parts in enumerate((sums, differences)):
                for outer, part in enumerate(butterfly(parts)):
                    at = (outer * 2 + core) * rows + number * chunk
                    mixed_ref[pl.ds(at, chunk), :] = part
                    mixed_ref[pl.ds(2 * SIDE * rows + at, chunk), :] = -part

    count = out_ref.shape[1]
    group = 16

    @pl.loop(0, count // group)
    def _(number):
        for lane in range(group):
            at = number * group + lane
            source = index_ref[step * count + at]
            out_ref[0, pl.ds(at, 1), :] = mixed_ref[pl.ds(source, 1), :]


def sampled_rows(index, own, other, scale):
    total = index.shape[0]
    count = total // SIDE
    rows = own.shape[1]
    return pl.pallas_call(
        functools.partial(sample_kernel, scale),
        grid_spec=pltpu.PrefetchScalarGridSpec(
            num_scalar_prefetch=1,
            grid=(SIDE,),
            in_specs=[
                pl.BlockSpec((SIDE, rows, LANE), lambda s, i: (0, 0, 0)),
                pl.BlockSpec((SIDE, rows, LANE), lambda s, i: (0, 0, 0)),
            ],
            out_specs=pl.BlockSpec((1, count, LANE), lambda s, i: (s, 0, 0)),
            scratch_shapes=[pltpu.VMEM((4 * SIDE * rows, LANE), jnp.float32)],
        ),
        out_shape=jax.ShapeDtypeStruct((SIDE, count, LANE), jnp.float32),
        compiler_params=pltpu.CompilerParams(vmem_limit_bytes=VMEM),
        cost_estimate=pl.CostEstimate(flops=2**24, bytes_accessed=2**24, transcendentals=0),
    )(index, own, other)


def gram_kernel(
    place_ref, mine_ref, sibling_ref, right_ref, left_ref, far_a_ref, far_b_ref, out_ref,
    left_high, left_low, right_high, right_low,
):
    me, core = place_ref[0], place_ref[1]
    step = pl.program_id(0)
    depth = mine_ref.shape[1]

    @pl.when(step == 0)
    def _():
        for distance, refs in enumerate(((mine_ref,), (right_ref,), (far_a_ref, far_b_ref), (left_ref,))):
            column = lax.rem(me + SIDE - distance, SIDE)
            at = 0
            for ref in refs:
                for number in range(ref.shape[0]):
                    high, low = split(ref[number])
                    left_high[column, at] = high
                    left_low[column, at] = low
                    at += 1
        for number in range(SIDE):
            mine, theirs = mine_ref[number], sibling_ref[number]
            zero = jnp.where(core == 0, mine, theirs)
            one = jnp.where(core == 0, theirs, mine)
            for part, value in enumerate((zero, one)):
                high, low = split(value)
                here = pl.ds((2 * number + part) * LANE, LANE)
                right_high[:, here] = high
                right_low[:, here] = low

    def block(ref, second):
        column = jnp.where(core == 0, second, step)
        number = jnp.where(core == 0, step, second)
        return ref[column, number]

    high = jnp.concatenate([block(left_high, second) for second in range(SIDE)], axis=1)
    low = jnp.concatenate([block(left_low, second) for second in range(SIDE)], axis=1)

    def product(a, b):
        return lax.dot_general(a, b, (((0,), (0,)), ((), ())), preferred_element_type=jnp.float32)

    wide = 256
    for number in range(right_high.shape[1] // wide):
        here = pl.ds(number * wide, wide)
        value = product(high, right_high[:, here])
        value += product(low, right_high[:, here])
        value += product(high, right_low[:, here])
        for second in range(SIDE):
            out_ref[0, second, :, here] = value[second * LANE : (second + 1) * LANE]


def gram_shares(where, mine, sibling, right, left, far_a, far_b):
    depth = mine.shape[1]
    width = 2 * SIDE * LANE

    def whole(array):
        return pl.BlockSpec(array.shape, lambda s, w: (0, 0, 0))

    operands = (mine, sibling, right, left, far_a, far_b)
    return pl.pallas_call(
        gram_kernel,
        grid_spec=pltpu.PrefetchScalarGridSpec(
            num_scalar_prefetch=1,
            grid=(SIDE,),
            in_specs=[whole(array) for array in operands],
            out_specs=pl.BlockSpec((1, SIDE, LANE, width), lambda s, w: (s, 0, 0, 0)),
            scratch_shapes=[
                pltpu.VMEM((SIDE, SIDE, depth, LANE), jnp.bfloat16),
                pltpu.VMEM((SIDE, SIDE, depth, LANE), jnp.bfloat16),
                pltpu.VMEM((depth, width), jnp.bfloat16),
                pltpu.VMEM((depth, width), jnp.bfloat16),
            ],
        ),
        out_shape=jax.ShapeDtypeStruct((SIDE, SIDE, LANE, width), jnp.float32),
        compiler_params=pltpu.CompilerParams(vmem_limit_bytes=VMEM),
        cost_estimate=pl.CostEstimate(flops=6 * 2**30, bytes_accessed=2**24, transcendentals=0),
    )(where, *operands)


def exchange(value, groups):
    return lax.all_to_all(value, "row", 0, 0, tiled=True, axis_index_groups=groups)


def row_index(wanted, z, y, core):
    rest = wanted.shape[0] // 16
    grid = wanted.reshape(NZ, NY, rest)
    grid = jnp.where(core == 0, grid, jnp.swapaxes(grid, 0, 1))
    inner = grid % 1024
    outer = grid // 1024
    outer_z, outer_y, outer_core = outer // 8, outer // 2 % 4, outer % 2
    first = jnp.where(core == 0, outer_y, outer_z)
    second = jnp.where(core == 0, outer_z, outer_y)
    both = second & jnp.where(core == 0, z, y)
    negative = (both ^ (both >> 1) ^ (outer_core & core)) & 1
    return (inner + 1024 * (first * 2 + outer_core) + 8192 * negative).reshape(-1).astype(jnp.int32)


def shards(design, signs, sample_rows):
    owned = sample_rows.shape[0]
    myself = lax.axis_index("row")
    column = lax.axis_index("col")
    z, y, core = myself // 8, myself // 2 % 4, myself % 2
    total = owned * lax.axis_size("row")
    scale = float(np.float32(1.0) / np.sqrt(np.float32(total)))

    table = jnp.asarray(hadamard(256), jnp.bfloat16)
    sign_column = signs.astype(jnp.float32)[:, None]
    sent = local_transform(design, sign_column, table, (1 - core).astype(jnp.int32)[None])
    kept = local_transform(design, sign_column, table, core.astype(jnp.int32)[None])
    swapped = lax.ppermute(sent, "row", SIBLING)
    wanted = lax.all_gather(sample_rows, "row", axis=0, tiled=True)
    index = row_index(wanted, z, y, core)

    own = exchange(kept, FIRST)
    other = exchange(swapped, FIRST)
    picked = sampled_rows(index, own, other, scale)
    arrived = exchange(picked, SECOND)
    summed = jnp.sum(arrived, axis=0).reshape(SIDE, 2 * owned, LANE)
    mine = exchange(summed, FIRST)

    right = lax.ppermute(mine, "col", around(1))
    left = lax.ppermute(mine, "col", around(3))
    far_a = lax.ppermute(right[: SIDE // 2], "col", around(1))
    far_b = lax.ppermute(left[SIDE // 2 :], "col", around(3))
    sibling = lax.ppermute(mine, "row", SIBLING)

    def rows_of(array):
        return lax.dynamic_slice_in_dim(array, core * owned, owned, 1)

    pair = jnp.stack([rows_of(mine), rows_of(sibling)])
    pair = jnp.where(core == 0, pair, pair[::-1])
    sketch = pair.transpose(2, 1, 0, 3).reshape(owned, 2 * SIDE * LANE)

    where = jnp.stack([column, core]).astype(jnp.int32)
    shares = gram_shares(where, mine, sibling, right, left, far_a, far_b)
    part = jnp.sum(exchange(shares, FIRST), axis=0)
    gram = jnp.sum(exchange(part, SECOND), axis=0)
    return (sketch, gram)


def solution(mesh):
    in_specs = (P("row", "col"), P("row"), P("row"))
    out_specs = (P("row", "col"), P("row", "col"))
    return jax.shard_map(shards, mesh=mesh, in_specs=in_specs, out_specs=out_specs, check_vma=False)
```

```python
import functools

import jax
import jax.numpy as jnp
import numpy as np
from jax import lax
from jax.experimental import pallas as pl
from jax.experimental.pallas import tpu as pltpu
from jax.sharding import PartitionSpec as P

SIDE = 4
LANE = 128
VMEM = 56 * 2**20


def place(z, y, c):
    return z * 8 + y * 2 + c


def partners(ring, step):
    pairs = []
    for z in range(SIDE):
        for y in range(SIDE):
            for c in range(2):
                along_y = c == ring
                other = (z, y ^ step) if along_y else (z ^ step, y)
                pairs.append((place(z, y, c), place(*other, c)))
    return pairs


FIRST, SECOND = 0, 1


def hop(value, ring, step):
    return lax.ppermute(value, "row", partners(ring, step))


def to_sibling(value):
    return lax.ppermute(value, "row", [(i, i ^ 1) for i in range(32)])


def across(value, step):
    return lax.ppermute(value, "row", [(i ^ 1, j) for i, j in partners(FIRST, step)])


def around(value, step):
    return lax.ppermute(value, "col", [(i, (i + step) % SIDE) for i in range(SIDE)])


def hadamard(order):
    index = np.arange(order)
    both = index[:, None] & index[None, :]
    count = np.zeros((order, order), np.int64)
    for bit in range(order.bit_length() - 1):
        count += both >> bit & 1
    return 1 - 2 * (count % 2)


def split(value):
    high = value.astype(jnp.bfloat16)
    low = (value - high.astype(jnp.float32)).astype(jnp.bfloat16)
    return high, low


def butterfly(parts):
    half = len(parts) // 2
    if half == 0:
        return parts
    low, high = butterfly(parts[:half]), butterfly(parts[half:])
    return [a + b for a, b in zip(low, high)] + [a - b for a, b in zip(low, high)]


def fixed(shape):
    return pl.BlockSpec(shape, lambda *_: (0,) * len(shape))


def f32(*shape):
    return jax.ShapeDtypeStruct(shape, jnp.float32)


def call(kernel, grid, in_specs, out_specs, out_shape, scalars=0, scratch=(), flops=2**24, moved=2**23):
    return pl.pallas_call(
        kernel,
        grid_spec=pltpu.PrefetchScalarGridSpec(
            num_scalar_prefetch=scalars,
            grid=grid,
            in_specs=in_specs,
            out_specs=out_specs,
            scratch_shapes=scratch,
        ),
        out_shape=out_shape,
        compiler_params=pltpu.CompilerParams(vmem_limit_bytes=VMEM),
        cost_estimate=pl.CostEstimate(flops=flops, bytes_accessed=moved, transcendentals=0),
    )


def local_kernel(_, table_ref, signs_ref, own_ref, other_ref, *refs):
    outs, held_ref, sems = refs[:-2], refs[-2], refs[-1]
    step = pl.program_id(0)
    size = table_ref.shape[0]
    parts = []
    for number in range(own_ref.shape[0] // size):
        rows = pl.ds(number * size, size)
        signed_table = table_ref[...] * signs_ref[:, rows].astype(jnp.bfloat16)
        high, low = split(jnp.concatenate([own_ref[rows, :], other_ref[rows, :]], axis=1))
        part = jnp.dot(signed_table, high, preferred_element_type=jnp.float32)
        parts.append(part + jnp.dot(signed_table, low, preferred_element_type=jnp.float32))
    for number, part in enumerate(butterfly(parts)):
        rows = pl.ds(number * size, size)
        held_ref[step, 0, rows, :] = part[:, :LANE]
        held_ref[step, 1, rows, :] = part[:, LANE:]

    def copy(k, side):
        return pltpu.make_async_copy(held_ref.at[k, side], outs[SIDE * side + k], sems.at[k, side])

    for k in range(SIDE):

        @pl.when(step == k)
        def _():
            copy(k, 0).start()
            copy(k, 1).start()

    @pl.when(step == SIDE - 1)
    def _():
        for k in range(SIDE):
            copy(k, 0).wait()
            copy(k, 1).wait()


def local_transform(where, design, signs, table):
    rows = design.shape[0]
    size = table.shape[0]
    return call(
        local_kernel,
        (SIDE,),
        [
            fixed((size, size)),
            fixed((1, rows)),
            pl.BlockSpec((rows, LANE), lambda k, w: (0, 2 * (w[1] ^ k) + w[0])),
            pl.BlockSpec((rows, LANE), lambda k, w: (0, 2 * (w[2] ^ k) + 1 - w[0])),
        ],
        [pl.BlockSpec(memory_space=pl.ANY)] * (2 * SIDE),
        [f32(rows, LANE)] * (2 * SIDE),
        scalars=1,
        scratch=[pltpu.VMEM((SIDE, 2, rows, LANE), jnp.float32), pltpu.SemaphoreType.DMA((SIDE, 2))],
        flops=2**30,
        moved=2**23,
    )(where, table, signs, design, design)


def sample_kernel(scale, chunk, owned, where_ref, index_ref, *refs):
    sources, outs = refs[: 2 * SIDE], refs[2 * SIDE : 3 * SIDE]
    mixed_ref, picked_ref, sems = refs[3 * SIDE :]
    step = pl.program_id(0)
    block = sources[0].shape[0]
    rows = block * pl.num_programs(0)
    size = 32

    @pl.loop(0, block // size)
    def _(number):
        here = pl.ds(pl.multiple_of(number * size, size), size)
        sums, differences = [], []
        for k in range(SIDE):
            own, other = sources[k][here, :] * scale, sources[SIDE + k][here, :] * scale
            sums.append(own + other)
            differences.append(own - other)
        for core, parts in enumerate((sums, differences)):
            for outer, part in enumerate(butterfly(parts)):
                at = (outer * 2 + core) * rows + step * block + number * size
                mixed_ref[pl.ds(pl.multiple_of(at, size), size), :] = part
                mixed_ref[pl.ds(pl.multiple_of(2 * SIDE * rows + at, size), size), :] = -part

    @pl.when(step == pl.num_programs(0) - 1)
    def _():
        core, first, second = where_ref[0], where_ref[1], where_ref[2]
        group = 64
        copies = []
        for m in (2, 1, 3, 0):
            for k in range(SIDE):
                outer, inner = jnp.where(core == 0, second ^ m, first ^ k), jnp.where(core == 0, first ^ k, second ^ m)
                start = (outer * 8 + inner * 2 + chunk) * owned

                @pl.loop(0, owned // group)
                def _(number):
                    for lane in range(group):
                        at = number * group + lane
                        picked_ref[m, pl.ds(k * owned + at, 1), :] = mixed_ref[pl.ds(index_ref[start + at], 1), :]

            copies.append(pltpu.make_async_copy(picked_ref.at[m], outs[m], sems.at[m]))
            copies[-1].start()
        for copy in copies:
            copy.wait()


def sampled_rows(where, index, sources, scale, chunk, owned):
    rows = sources[0].shape[0]
    steps = 2
    return call(
        functools.partial(sample_kernel, scale, chunk, owned),
        (steps,),
        [pl.BlockSpec((rows // steps, LANE), lambda s, w, i: (s, 0))] * (2 * SIDE),
        [pl.BlockSpec(memory_space=pl.ANY)] * SIDE,
        [f32(SIDE * owned, LANE)] * SIDE,
        scalars=2,
        scratch=[
            pltpu.VMEM((4 * SIDE * rows, LANE), jnp.float32),
            pltpu.VMEM((SIDE, SIDE * owned, LANE), jnp.float32),
            pltpu.SemaphoreType.DMA((SIDE,)),
        ],
    )(where, index, *sources)


def rows_sum_kernel(*refs):
    sources, outs = refs[:SIDE], refs[SIDE:]
    owned = outs[0].shape[0]
    for k, out_ref in enumerate(outs):
        here = pl.ds(k * owned, owned)
        out_ref[...] = (sources[0][here, :] + sources[1][here, :]) + (sources[2][here, :] + sources[3][here, :])


def rows_sum(*operands):
    owned = operands[0].shape[0] // SIDE
    return call(
        rows_sum_kernel,
        (),
        [fixed(operand.shape) for operand in operands],
        [fixed((owned, LANE))] * SIDE,
        [f32(owned, LANE)] * SIDE,
    )(*operands)


def sketch_kernel(where_ref, mine_zero, mine_one, sibling_zero, sibling_one, out_ref):
    core, first, second = where_ref[0], where_ref[1], where_ref[2]
    for step in range(SIDE):
        mine = jnp.where(core == 0, mine_zero[step], mine_one[step])
        theirs = jnp.where(core == 0, sibling_zero[step], sibling_one[step])
        for block, value in ((2 * (first ^ step) + core, mine), (2 * (second ^ step) + 1 - core, theirs)):
            out_ref[:, pl.ds(pl.multiple_of(block * LANE, LANE), LANE)] = value


def sketch_rows(where, *operands):
    owned = operands[0].shape[1]
    width = 2 * SIDE * LANE
    return call(
        sketch_kernel,
        (1,),
        [fixed(operand.shape) for operand in operands],
        fixed((owned, width)),
        f32(owned, width),
        scalars=1,
    )(where, *operands)


def gram_kernel(half, plan, where_ref, *refs):
    inputs, outs = refs[:12], refs[12 : 12 + len(plan)]
    right_in, left_in, *held, right_sems, left_sems, out_sems = refs[12 + len(plan) :]
    core, first, second, me = (where_ref[i] for i in range(4))
    owned = right_in.shape[0] // 2
    blocks = [(number, block) for number, entries in enumerate(plan) for block in entries]

    def right_copy(chunk, number, side):
        mine, sibling = inputs[6 * chunk], inputs[6 * chunk + 1]
        j = 2 * half + number
        source = (mine.at[first ^ j], sibling.at[second ^ j])[side]
        block = 2 * number + jnp.where(side == 0, core, 1 - core)
        rows, lanes = pl.ds(chunk * owned, owned), pl.ds(pl.multiple_of(block * LANE, LANE), LANE)
        return pltpu.make_async_copy(source, right_in.at[rows, lanes], right_sems.at[chunk, number, side])

    rights = [right_copy(chunk, number, side) for chunk in range(2) for number in range(2) for side in range(2)]
    for copy in rights:
        copy.start()
    lefts = []
    for slot, (_, (k, m)) in enumerate(blocks):
        column = jnp.where(core == 0, second ^ m, first ^ k)
        step = jnp.where(core == 0, k, first ^ second ^ m)
        distance = lax.rem(me + SIDE - column, SIDE)
        for chunk in range(2):
            mine, _, right, left, far_a, far_b = inputs[6 * chunk : 6 * chunk + 6]
            target = left_in.at[slot, pl.ds(chunk * owned, owned), :]
            sem = left_sems.at[slot, chunk]
            cases = [(distance == 0, mine, step), (distance == 1, right, step), (distance == 3, left, step)]
            cases.append(((distance == 2) & (step < 2), far_a, jnp.minimum(step, 1)))
            cases.append(((distance == 2) & (step >= 2), far_b, jnp.maximum(step, 2) - 2))
            for chosen, ref, at in cases:

                @pl.when(chosen)
                def _():
                    pltpu.make_async_copy(ref.at[at], target, sem).start()

            lefts.append(pltpu.make_async_copy(mine.at[0], target, sem))

    def product(a, b):
        return lax.dot_general(a, b, (((0,), (0,)), ((), ())), preferred_element_type=jnp.float32)

    for copy in rights:
        copy.wait()
    right_high, right_low = split(right_in[...])
    group = 4
    copies = []
    done = [0] * len(plan)
    for base in range(0, len(blocks), group):
        for copy in lefts[2 * base : 2 * (base + group)]:
            copy.wait()
        high, low = split(jnp.concatenate([left_in[base + i] for i in range(group)], axis=1))
        value = product(high, right_high) + product(low, right_high) + product(high, right_low)
        for i in range(group):
            number = blocks[base + i][0]
            held[number][done[number]] = value[i * LANE : (i + 1) * LANE]
            done[number] += 1
            if done[number] == len(plan[number]):
                copies.append(pltpu.make_async_copy(held[number], outs[number], out_sems.at[number]))
                copies[-1].start()
    for copy in copies:
        copy.wait()


def gram_shares(where, operands, half, plan):
    owned = operands[0].shape[1]
    wide = SIDE * LANE
    shapes = [(len(entries), LANE, wide) for entries in plan]
    slots = sum(len(entries) for entries in plan)
    return call(
        functools.partial(gram_kernel, half, plan),
        (),
        [pl.BlockSpec(memory_space=pltpu.SMEM)] + [pl.BlockSpec(memory_space=pl.ANY)] * len(operands),
        [pl.BlockSpec(memory_space=pl.ANY)] * len(plan),
        [f32(*shape) for shape in shapes],
        scratch=[
            pltpu.VMEM((2 * owned, wide), jnp.float32),
            pltpu.VMEM((slots, 2 * owned, LANE), jnp.float32),
            *[pltpu.VMEM(shape, jnp.float32) for shape in shapes],
            pltpu.SemaphoreType.DMA((2, 2, 2)),
            pltpu.SemaphoreType.DMA((slots, 2)),
            pltpu.SemaphoreType.DMA((len(plan),)),
        ],
        flops=3 * 2**29,
        moved=5 * 2**20,
    )(where, *operands)


def ring_sum_kernel(kept_ref, from_one, from_three, last_one, last_three, *outs):
    for side, (early, late) in enumerate(((from_one, last_three), (from_three, last_one))):
        for part in range(2):
            outs[2 * side + part][...] = kept_ref[2 * side + part] + early[2 + part] + late[part]


def ring_sum(*operands):
    wide = operands[0].shape[-1]
    return call(
        ring_sum_kernel,
        (),
        [fixed(operand.shape) for operand in operands],
        [fixed((LANE, wide))] * SIDE,
        [f32(LANE, wide)] * SIDE,
    )(*operands)


def combine_kernel(*refs):
    out_ref = refs[-1]
    wide = refs[0].shape[1]
    for half in range(2):
        a, b, c, d = refs[SIDE * half : SIDE * half + SIDE]
        out_ref[:, pl.ds(half * wide, wide)] = (a[...] + b[...]) + (c[...] + d[...])


def combine(*operands):
    rows, wide = operands[0].shape
    return call(
        combine_kernel,
        (),
        [fixed(operand.shape) for operand in operands],
        fixed((rows, 2 * wide)),
        f32(rows, 2 * wide),
    )(*operands)


def sample_index(sample_rows, z, y, core):
    groups = lax.axis_size("row")
    spread = jnp.broadcast_to(sample_rows, (groups, sample_rows.shape[0]))
    wanted = lax.all_to_all(spread, "row", 0, 0, tiled=True).reshape(-1)
    first_here, second_here = jnp.where(core == 0, y, z), jnp.where(core == 0, z, y)
    inner, outer = wanted % 1024, wanted // 1024
    outer_z, outer_y, outer_core = outer // 8, outer // 2 % 4, outer % 2
    first = jnp.where(core == 0, outer_y, outer_z)
    second = jnp.where(core == 0, outer_z, outer_y)
    both = (first & first_here) ^ (second & second_here)
    negative = (both ^ (both >> 1) ^ (outer_core & core)) & 1
    return (inner + 1024 * (first * 2 + outer_core) + 8192 * negative).astype(jnp.int32)


def shards(design, signs, sample_rows):
    owned = sample_rows.shape[0]
    myself = lax.axis_index("row")
    column = lax.axis_index("col")
    z, y, core = myself // 8, myself // 2 % 4, myself % 2
    first, second = jnp.where(core == 0, y, z), jnp.where(core == 0, z, y)
    where = jnp.stack([core, first, second, column]).astype(jnp.int32)
    total = owned * lax.axis_size("row")
    scale = float(np.float32(1.0) / np.sqrt(np.float32(total)))

    table = jnp.asarray(hadamard(256), jnp.bfloat16)
    index = sample_index(sample_rows, z, y, core)
    pieces = local_transform(where, design, signs[None, :], table)
    sources = [pieces[0]] + [hop(pieces[step], FIRST, step) for step in (1, 2, 3)]
    sources += [across(pieces[SIDE + step], step) for step in range(SIDE)]

    gathered = []
    for chunk in range(2):
        picked = sampled_rows(where, index, sources, scale, chunk, owned)
        sums = rows_sum(picked[0], *[hop(picked[step], SECOND, step) for step in (1, 2, 3)])
        mine = jnp.stack([sums[0]] + [hop(sums[step], FIRST, step) for step in (1, 2, 3)])
        right, left = around(mine, 1), around(mine, 3)
        far_a, far_b = around(right[: SIDE // 2], 1), around(left[SIDE // 2 :], 3)
        gathered.append((mine, to_sibling(mine), right, left, far_a, far_b))

    sketch = sketch_rows(where, gathered[0][0], gathered[1][0], gathered[0][1], gathered[1][1])

    operands = gathered[0] + gathered[1]
    low, high = (0, 1), (2, 3)

    def blocks(*entries):
        return [(first, second) for first, seconds in entries for second in seconds]

    early = [gram_shares(where, operands, half, [blocks((2, low), (1, low)), blocks((2, high), (3, high))]) for half in range(2)]
    late_plan = [blocks((1, high)), blocks((3, low)), blocks((0, low), (0, high))]
    late = [gram_shares(where, operands, half, late_plan) for half in range(2)]
    parts = []
    for (to_one, to_three), (rest_one, rest_three, here) in zip(early, late):
        from_one, from_three = hop(to_one, FIRST, 1), hop(to_three, FIRST, 3)
        last_one = hop(rest_one + from_three[:2], FIRST, 1)
        last_three = hop(rest_three + from_one[:2], FIRST, 3)
        sums = ring_sum(here, from_one, from_three, last_one, last_three)
        parts += [sums[0]] + [hop(sums[step], SECOND, step) for step in (1, 2, 3)]
    return (sketch, combine(*parts))


def solution(mesh):
    in_specs = (P("row", "col"), P("row"), P("row"))
    out_specs = (P("row", "col"), P("row", "col"))
    return jax.shard_map(shards, mesh=mesh, in_specs=in_specs, out_specs=out_specs, check_vma=False)
```

```python
import functools

import jax
import jax.numpy as jnp
import numpy as np
from jax import lax
from jax.experimental import pallas as pl
from jax.experimental.pallas import tpu as pltpu
from jax.sharding import PartitionSpec as P

SIDE = 4
LANE = 128
VMEM = 56 * 2**20


def place(z, y, c):
    return z * 8 + y * 2 + c


def partners(ring, step):
    pairs = []
    for z in range(SIDE):
        for y in range(SIDE):
            for c in range(2):
                along_y = c == ring
                other = (z, y ^ step) if along_y else (z ^ step, y)
                pairs.append((place(z, y, c), place(*other, c)))
    return pairs


FIRST, SECOND = 0, 1
CUTS = (0, 512, 1024)


def groups(ring):
    lines = []
    for fixed_at in range(SIDE):
        for c in range(2):
            along_y = c == ring
            lines.append([place(fixed_at, i, c) if along_y else place(i, fixed_at, c) for i in range(SIDE)])
    return lines


def exchange(value, ring):
    return lax.all_to_all(value, "row", 0, 0, tiled=True, axis_index_groups=groups(ring))


def hop(value, ring, step):
    return lax.ppermute(value, "row", partners(ring, step))


def to_sibling(value):
    return lax.ppermute(value, "row", [(i, i ^ 1) for i in range(32)])


def across(value, step):
    return lax.ppermute(value, "row", [(i ^ 1, j) for i, j in partners(FIRST, step)])


def around(value, step):
    return lax.ppermute(value, "col", [(i, (i + step) % SIDE) for i in range(SIDE)])


def hadamard(order):
    index = np.arange(order)
    both = index[:, None] & index[None, :]
    count = np.zeros((order, order), np.int64)
    for bit in range(order.bit_length() - 1):
        count += both >> bit & 1
    return 1 - 2 * (count % 2)


def split(value):
    high = value.astype(jnp.bfloat16)
    low = (value - high.astype(jnp.float32)).astype(jnp.bfloat16)
    return high, low


def butterfly(parts):
    half = len(parts) // 2
    if half == 0:
        return parts
    low, high = butterfly(parts[:half]), butterfly(parts[half:])
    return [a + b for a, b in zip(low, high)] + [a - b for a, b in zip(low, high)]


def fixed(shape):
    return pl.BlockSpec(shape, lambda *_: (0,) * len(shape))


def f32(*shape):
    return jax.ShapeDtypeStruct(shape, jnp.float32)


def call(kernel, grid, in_specs, out_specs, out_shape, scalars=0, scratch=(), flops=2**24, moved=2**23):
    return pl.pallas_call(
        kernel,
        grid_spec=pltpu.PrefetchScalarGridSpec(
            num_scalar_prefetch=scalars,
            grid=grid,
            in_specs=in_specs,
            out_specs=out_specs,
            scratch_shapes=scratch,
        ),
        out_shape=out_shape,
        compiler_params=pltpu.CompilerParams(vmem_limit_bytes=VMEM),
        cost_estimate=pl.CostEstimate(flops=flops, bytes_accessed=moved, transcendentals=0),
    )


def local_kernel(_, table_ref, signs_ref, own_ref, other_ref, *refs):
    outs, held_ref, sems = refs[:-2], refs[-2], refs[-1]
    step = pl.program_id(0)
    size = table_ref.shape[0]
    parts = []
    for number in range(own_ref.shape[0] // size):
        rows = pl.ds(number * size, size)
        signed_table = table_ref[...] * signs_ref[:, rows].astype(jnp.bfloat16)
        high, low = split(jnp.concatenate([own_ref[rows, :], other_ref[rows, :]], axis=1))
        part = jnp.dot(signed_table, high, preferred_element_type=jnp.float32)
        parts.append(part + jnp.dot(signed_table, low, preferred_element_type=jnp.float32))
    for number, part in enumerate(butterfly(parts)):
        rows = pl.ds(number * size, size)
        held_ref[step, 0, rows, :] = part[:, :LANE]
        held_ref[step, 1, rows, :] = part[:, LANE:]

    def copy(k, side):
        return pltpu.make_async_copy(held_ref.at[k, side], outs[SIDE * side + k], sems.at[k, side])

    for k in range(SIDE):

        @pl.when(step == k)
        def _():
            copy(k, 0).start()
            copy(k, 1).start()

    @pl.when(step == SIDE - 1)
    def _():
        for k in range(SIDE):
            copy(k, 0).wait()
            copy(k, 1).wait()


def local_transform(where, design, signs, table):
    rows = design.shape[0]
    size = table.shape[0]
    return call(
        local_kernel,
        (SIDE,),
        [
            fixed((size, size)),
            fixed((1, rows)),
            pl.BlockSpec((rows, LANE), lambda k, w: (0, 2 * (w[1] ^ k) + w[0])),
            pl.BlockSpec((rows, LANE), lambda k, w: (0, 2 * (w[2] ^ k) + 1 - w[0])),
        ],
        [pl.BlockSpec(memory_space=pl.ANY)] * (2 * SIDE),
        [f32(rows, LANE)] * (2 * SIDE),
        scalars=1,
        scratch=[pltpu.VMEM((SIDE, 2, rows, LANE), jnp.float32), pltpu.SemaphoreType.DMA((SIDE, 2))],
        flops=2**30,
        moved=2**23,
    )(where, table, signs, design, design)


def sample_kernel(scale, chunk, owned, where_ref, index_ref, *refs):
    sources, outs = refs[: 2 * SIDE], refs[2 * SIDE : 3 * SIDE]
    mixed_ref, picked_ref, sems = refs[3 * SIDE :]
    step = pl.program_id(0)
    block = sources[0].shape[0]
    rows = block * pl.num_programs(0)
    size = 32

    @pl.loop(0, block // size)
    def _(number):
        here = pl.ds(pl.multiple_of(number * size, size), size)
        sums, differences = [], []
        for k in range(SIDE):
            own, other = sources[k][here, :] * scale, sources[SIDE + k][here, :] * scale
            sums.append(own + other)
            differences.append(own - other)
        for core, parts in enumerate((sums, differences)):
            for outer, part in enumerate(butterfly(parts)):
                at = (outer * 2 + core) * rows + step * block + number * size
                mixed_ref[pl.ds(pl.multiple_of(at, size), size), :] = part
                mixed_ref[pl.ds(pl.multiple_of(2 * SIDE * rows + at, size), size), :] = -part

    @pl.when(step == pl.num_programs(0) - 1)
    def _():
        core, second = where_ref[0], where_ref[2]
        group = 64
        copies = []
        for m in (2, 1, 3, 0):
            for k in range(SIDE):
                outer, inner = jnp.where(core == 0, second ^ m, k), jnp.where(core == 0, k, second ^ m)
                start = (outer * 8 + inner * 2 + chunk) * owned

                @pl.loop(0, owned // group)
                def _(number):
                    for lane in range(group):
                        at = number * group + lane
                        picked_ref[m, k, pl.ds(at, 1), :] = mixed_ref[pl.ds(index_ref[start + at], 1), :]

            copies.append(pltpu.make_async_copy(picked_ref.at[m], outs[m], sems.at[m]))
            copies[-1].start()
        for copy in copies:
            copy.wait()


def sampled_rows(where, index, sources, scale, chunk, owned):
    rows = sources[0].shape[0]
    steps = 2
    return call(
        functools.partial(sample_kernel, scale, chunk, owned),
        (steps,),
        [pl.BlockSpec((rows // steps, LANE), lambda s, w, i: (s, 0))] * (2 * SIDE),
        [pl.BlockSpec(memory_space=pl.ANY)] * SIDE,
        [f32(SIDE, owned, LANE)] * SIDE,
        scalars=2,
        scratch=[
            pltpu.VMEM((4 * SIDE * rows, LANE), jnp.float32),
            pltpu.VMEM((SIDE, SIDE, owned, LANE), jnp.float32),
            pltpu.SemaphoreType.DMA((SIDE,)),
        ],
    )(where, index, *sources)


def sketch_kernel(where_ref, mine_zero, mine_one, sibling_zero, sibling_one, out_ref):
    core = where_ref[0]
    for j in range(SIDE):
        mine = jnp.where(core == 0, mine_zero[j], mine_one[j])
        theirs = jnp.where(core == 0, sibling_zero[j], sibling_one[j])
        out_ref[:, pl.ds(2 * j * LANE, LANE)] = jnp.where(core == 0, mine, theirs)
        out_ref[:, pl.ds((2 * j + 1) * LANE, LANE)] = jnp.where(core == 0, theirs, mine)


def sketch_rows(where, *operands):
    owned = operands[0].shape[1]
    width = 2 * SIDE * LANE
    return call(
        sketch_kernel,
        (1,),
        [fixed(operand.shape) for operand in operands],
        fixed((owned, width)),
        f32(owned, width),
        scalars=1,
    )(where, *operands)


def gram_kernel(plan, where_ref, *refs):
    inputs, outs = refs[:12], refs[12 : 12 + 2 * len(plan)]
    right_in, left_in, *held, right_sems, left_sems, out_sems = refs[12 + 2 * len(plan) :]
    core, first, second, me = (where_ref[i] for i in range(4))
    owned = right_in.shape[0] // 2
    blocks = [(number, block) for number, entries in enumerate(plan) for block in entries]

    def right_copy(chunk, j, side):
        source = inputs[6 * chunk + side].at[j]
        block = 2 * j + jnp.where(side == 0, core, 1 - core)
        rows, lanes = pl.ds(chunk * owned, owned), pl.ds(pl.multiple_of(block * LANE, LANE), LANE)
        return pltpu.make_async_copy(source, right_in.at[rows, lanes], right_sems.at[chunk, j, side])

    rights = [right_copy(chunk, j, side) for chunk in range(2) for j in range(SIDE) for side in range(2)]
    for copy in rights:
        copy.start()
    lefts = []
    for slot, (_, (k, m)) in enumerate(blocks):
        column = jnp.where(core == 0, second ^ m, first ^ k)
        j = jnp.where(core == 0, first ^ k, second ^ m)
        distance = lax.rem(me + SIDE - column, SIDE)
        for chunk in range(2):
            mine, _, right, left, far_a, far_b = inputs[6 * chunk : 6 * chunk + 6]
            target = left_in.at[slot, pl.ds(chunk * owned, owned), :]
            sem = left_sems.at[slot, chunk]
            cases = [(distance == 0, mine, j), (distance == 1, right, j), (distance == 3, left, j)]
            cases.append(((distance == 2) & (j < 2), far_a, jnp.minimum(j, 1)))
            cases.append(((distance == 2) & (j >= 2), far_b, jnp.maximum(j, 2) - 2))
            for chosen, ref, at in cases:

                @pl.when(chosen)
                def _():
                    pltpu.make_async_copy(ref.at[at], target, sem).start()

            lefts.append(pltpu.make_async_copy(mine.at[0], target, sem))

    def product(a, b):
        return lax.dot_general(a, b, (((0,), (0,)), ((), ())), preferred_element_type=jnp.float32)

    for copy in rights:
        copy.wait()
    right_high, right_low = split(right_in[...])
    group = 4
    copies = []
    done = [0] * len(plan)
    for base in range(0, len(blocks), group):
        for copy in lefts[2 * base : 2 * (base + group)]:
            copy.wait()
        high, low = split(jnp.concatenate([left_in[base + i] for i in range(group)], axis=1))
        for half in range(2):
            here = slice(CUTS[half], CUTS[half + 1])
            value = product(high, right_high[:, here]) + product(low, right_high[:, here])
            value += product(high, right_low[:, here])
            at = list(done)
            for i in range(group):
                number = blocks[base + i][0]
                slot = 2 * number + half
                held[slot][at[number]] = value[i * LANE : (i + 1) * LANE]
                at[number] += 1
                if at[number] == len(plan[number]):
                    copies.append(pltpu.make_async_copy(held[slot], outs[slot], out_sems.at[slot]))
                    copies[-1].start()
        done = at
    for copy in copies:
        copy.wait()


def gram_shares(where, operands, plan):
    owned = operands[0].shape[1]
    shapes = [(len(entries), LANE, CUTS[half + 1] - CUTS[half]) for entries in plan for half in range(2)]
    slots = sum(len(entries) for entries in plan)
    return call(
        functools.partial(gram_kernel, plan),
        (),
        [pl.BlockSpec(memory_space=pltpu.SMEM)] + [pl.BlockSpec(memory_space=pl.ANY)] * len(operands),
        [pl.BlockSpec(memory_space=pl.ANY)] * len(shapes),
        [f32(*shape) for shape in shapes],
        scratch=[
            pltpu.VMEM((2 * owned, CUTS[-1]), jnp.float32),
            pltpu.VMEM((slots, 2 * owned, LANE), jnp.float32),
            *[pltpu.VMEM(shape, jnp.float32) for shape in shapes],
            pltpu.SemaphoreType.DMA((2, SIDE, 2)),
            pltpu.SemaphoreType.DMA((slots, 2)),
            pltpu.SemaphoreType.DMA((len(shapes),)),
        ],
        flops=3 * 2**30,
        moved=2**23,
    )(where, *operands)


def sample_index(sample_rows, z, y, core):
    groups = lax.axis_size("row")
    spread = jnp.broadcast_to(sample_rows, (groups, sample_rows.shape[0]))
    wanted = lax.all_to_all(spread, "row", 0, 0, tiled=True).reshape(-1)
    first_here, second_here = jnp.where(core == 0, y, z), jnp.where(core == 0, z, y)
    inner, outer = wanted % 1024, wanted // 1024
    outer_z, outer_y, outer_core = outer // 8, outer // 2 % 4, outer % 2
    first = jnp.where(core == 0, outer_y, outer_z)
    second = jnp.where(core == 0, outer_z, outer_y)
    both = (first & first_here) ^ (second & second_here)
    negative = (both ^ (both >> 1) ^ (outer_core & core)) & 1
    return (inner + 1024 * (first * 2 + outer_core) + 8192 * negative).astype(jnp.int32)


def shards(design, signs, sample_rows):
    owned = sample_rows.shape[0]
    myself = lax.axis_index("row")
    column = lax.axis_index("col")
    z, y, core = myself // 8, myself // 2 % 4, myself % 2
    first, second = jnp.where(core == 0, y, z), jnp.where(core == 0, z, y)
    where = jnp.stack([core, first, second, column]).astype(jnp.int32)
    total = owned * lax.axis_size("row")
    scale = float(np.float32(1.0) / np.sqrt(np.float32(total)))

    table = jnp.asarray(hadamard(256), jnp.bfloat16)
    pieces = local_transform(where, design, signs[None, :], table)
    own, theirs = pieces[:SIDE], list(pieces[SIDE:])
    sample_rows, _ = lax.optimization_barrier((sample_rows, own[0]))
    index = sample_index(sample_rows, z, y, core)
    index, theirs[0], theirs[3] = lax.optimization_barrier((index, theirs[0], theirs[3]))
    sources = [own[0]] + [hop(own[step], FIRST, step) for step in (1, 2, 3)]
    sources += [across(theirs[step], step) for step in range(SIDE)]

    gathered = []
    for chunk in range(2):
        picked = sampled_rows(where, index, sources, scale, chunk, owned)
        arrived = [hop(picked[step], SECOND, step) for step in (1, 2, 3)]
        sums = (picked[0] + arrived[0]) + (arrived[1] + arrived[2])
        mine = exchange(sums, FIRST)
        if gathered:
            mine, *_ = lax.optimization_barrier((mine, gathered[0][2], gathered[0][3]))
        right, left = around(mine, 1), around(mine, 3)
        far_a, far_b = around(right[: SIDE // 2], 1), around(left[SIDE // 2 :], 3)
        gathered.append((mine, to_sibling(mine), right, left, far_a, far_b))

    sketch = sketch_rows(where, gathered[0][0], gathered[1][0], gathered[0][1], gathered[1][1])

    operands = gathered[0] + gathered[1]
    low, high = (0, 1), (2, 3)

    def blocks(*entries):
        return [(first, second) for first, seconds in entries for second in seconds]

    early = gram_shares(where, operands, [blocks((2, low), (1, low)), blocks((2, high), (3, high))])
    late = gram_shares(where, operands, [blocks((1, high)), blocks((3, low)), blocks((0, low), (0, high))])
    parts = []
    for half in range(2):
        to_one, to_three = early[half::2]
        rest_one, rest_three, here = late[half::2]
        from_one, from_three = hop(to_one, FIRST, 1), hop(to_three, FIRST, 3)
        last_one = hop(rest_one + from_three[:2], FIRST, 1)
        last_three = hop(rest_three + from_one[:2], FIRST, 3)
        sums = [here[0] + from_one[2] + last_three[0], here[1] + from_one[3] + last_three[1]]
        sums += [here[2] + from_three[2] + last_one[0], here[3] + from_three[3] + last_one[1]]
        arrived = [hop(sums[step], SECOND, step) for step in (1, 2, 3)]
        parts.append((sums[0] + arrived[0]) + (arrived[1] + arrived[2]))
    return (sketch, jnp.concatenate(parts, axis=1))


def solution(mesh):
    in_specs = (P("row", "col"), P("row"), P("row"))
    out_specs = (P("row", "col"), P("row", "col"))
    return jax.shard_map(shards, mesh=mesh, in_specs=in_specs, out_specs=out_specs, check_vma=False)
```

```python
import functools

import jax
import jax.numpy as jnp
import numpy as np
from jax import lax
from jax.experimental import pallas as pl
from jax.experimental.pallas import tpu as pltpu
from jax.sharding import PartitionSpec as P

SIDE = 4
LANE = 128
VMEM = 40 * 2**20


def place(z, y, c):
    return z * 8 + y * 2 + c


def partners(ring, step):
    pairs = []
    for z in range(SIDE):
        for y in range(SIDE):
            for c in range(2):
                along_y = c == ring
                other = (z, y ^ step) if along_y else (z ^ step, y)
                pairs.append((place(z, y, c), place(*other, c)))
    return pairs


FIRST, SECOND = 0, 1
CUTS = (0, 512, 1024)


def groups(ring):
    lines = []
    for fixed_at in range(SIDE):
        for c in range(2):
            along_y = c == ring
            lines.append([place(fixed_at, i, c) if along_y else place(i, fixed_at, c) for i in range(SIDE)])
    return lines


def exchange(value, ring):
    return lax.all_to_all(value, "row", 0, 0, tiled=True, axis_index_groups=groups(ring))


def hop(value, ring, step):
    return lax.ppermute(value, "row", partners(ring, step))


def to_sibling(value):
    return lax.ppermute(value, "row", [(i, i ^ 1) for i in range(32)])


def across(value, step):
    return lax.ppermute(value, "row", [(i ^ 1, j) for i, j in partners(FIRST, step)])


def around(value, step):
    return lax.ppermute(value, "col", [(i, (i + step) % SIDE) for i in range(SIDE)])


def hadamard(order):
    index = np.arange(order)
    both = index[:, None] & index[None, :]
    count = np.zeros((order, order), np.int64)
    for bit in range(order.bit_length() - 1):
        count += both >> bit & 1
    return 1 - 2 * (count % 2)


def split(value):
    high = value.astype(jnp.bfloat16)
    low = (value - high.astype(jnp.float32)).astype(jnp.bfloat16)
    return high, low


def butterfly(parts):
    half = len(parts) // 2
    if half == 0:
        return parts
    low, high = butterfly(parts[:half]), butterfly(parts[half:])
    return [a + b for a, b in zip(low, high)] + [a - b for a, b in zip(low, high)]


def fixed(shape):
    return pl.BlockSpec(shape, lambda *_: (0,) * len(shape))


def f32(*shape):
    return jax.ShapeDtypeStruct(shape, jnp.float32)


def call(kernel, grid, in_specs, out_specs, out_shape, scalars=0, scratch=(), flops=2**24, moved=2**23, vmem=VMEM):
    return pl.pallas_call(
        kernel,
        grid_spec=pltpu.PrefetchScalarGridSpec(
            num_scalar_prefetch=scalars,
            grid=grid,
            in_specs=in_specs,
            out_specs=out_specs,
            scratch_shapes=scratch,
        ),
        out_shape=out_shape,
        compiler_params=pltpu.CompilerParams(vmem_limit_bytes=vmem),
        cost_estimate=pl.CostEstimate(flops=flops, bytes_accessed=moved, transcendentals=0),
    )


def local_kernel(_, table_ref, signs_ref, own_ref, other_ref, *refs):
    outs, held_ref, sems = refs[:-2], refs[-2], refs[-1]
    step = pl.program_id(0)
    size = table_ref.shape[0]
    parts = []
    for number in range(own_ref.shape[0] // size):
        rows = pl.ds(number * size, size)
        signed_table = table_ref[...] * signs_ref[:, rows].astype(jnp.bfloat16)
        high, low = split(jnp.concatenate([own_ref[rows, :], other_ref[rows, :]], axis=1))
        part = jnp.dot(signed_table, high, preferred_element_type=jnp.float32)
        parts.append(part + jnp.dot(signed_table, low, preferred_element_type=jnp.float32))
    for number, part in enumerate(butterfly(parts)):
        rows = pl.ds(number * size, size)
        held_ref[step, 0, rows, :] = part[:, :LANE]
        held_ref[step, 1, rows, :] = part[:, LANE:]

    def copy(k, side):
        return pltpu.make_async_copy(held_ref.at[k, side], outs[SIDE * side + k], sems.at[k, side])

    for k in range(SIDE):

        @pl.when(step == k)
        def _():
            copy(k, 0).start()
            copy(k, 1).start()

    @pl.when(step == SIDE - 1)
    def _():
        for k in range(SIDE):
            copy(k, 0).wait()
            copy(k, 1).wait()


def local_transform(where, design, signs, table):
    rows = design.shape[0]
    size = table.shape[0]
    return call(
        local_kernel,
        (SIDE,),
        [
            fixed((size, size)),
            fixed((1, rows)),
            pl.BlockSpec((rows, LANE), lambda k, w: (0, 2 * (w[1] ^ k) + w[0])),
            pl.BlockSpec((rows, LANE), lambda k, w: (0, 2 * (w[2] ^ k) + 1 - w[0])),
        ],
        [pl.BlockSpec(memory_space=pl.ANY)] * (2 * SIDE),
        [f32(rows, LANE)] * (2 * SIDE),
        scalars=1,
        scratch=[pltpu.VMEM((SIDE, 2, rows, LANE), jnp.float32), pltpu.SemaphoreType.DMA((SIDE, 2))],
        flops=2**30,
        moved=2**23,
        vmem=60 * 2**20,
    )(where, table, signs, design, design)


def sample_kernel(scale, chunk, owned, where_ref, index_ref, *refs):
    sources, outs = refs[: 2 * SIDE], refs[2 * SIDE : 3 * SIDE]
    mixed_ref, picked_ref, sems = refs[3 * SIDE :]
    rows = sources[0].shape[0]
    size = 32

    @pl.loop(0, rows // size)
    def _(number):
        here = pl.ds(pl.multiple_of(number * size, size), size)
        sums, differences = [], []
        for k in range(SIDE):
            own, other = sources[k][here, :] * scale, sources[SIDE + k][here, :] * scale
            sums.append(own + other)
            differences.append(own - other)
        for core, parts in enumerate((sums, differences)):
            for outer, part in enumerate(butterfly(parts)):
                at = (outer * 2 + core) * rows + number * size
                mixed_ref[pl.ds(pl.multiple_of(at, size), size), :] = part
                mixed_ref[pl.ds(pl.multiple_of(2 * SIDE * rows + at, size), size), :] = -part

    core, second = where_ref[0], where_ref[2]
    group = 64
    copies = []
    for m in (2, 1, 3, 0):
        for k in range(SIDE):
            outer, inner = jnp.where(core == 0, second ^ m, k), jnp.where(core == 0, k, second ^ m)
            start = (outer * 8 + inner * 2 + chunk) * owned

            @pl.loop(0, owned // group)
            def _(number):
                for lane in range(group):
                    at = number * group + lane
                    picked_ref[m, k, pl.ds(at, 1), :] = mixed_ref[pl.ds(index_ref[start + at], 1), :]

        copies.append(pltpu.make_async_copy(picked_ref.at[m], outs[m], sems.at[m]))
        copies[-1].start()
    for copy in copies:
        copy.wait()


def sampled_rows(where, index, sources, scale, chunk, owned):
    rows = sources[0].shape[0]
    return call(
        functools.partial(sample_kernel, scale, chunk, owned),
        (),
        [pl.BlockSpec(memory_space=pltpu.SMEM)] * 2 + [pl.BlockSpec(memory_space=pltpu.VMEM)] * (2 * SIDE),
        [pl.BlockSpec(memory_space=pl.ANY)] * SIDE,
        [f32(SIDE, owned, LANE)] * SIDE,
        scratch=[
            pltpu.VMEM((4 * SIDE * rows, LANE), jnp.float32),
            pltpu.VMEM((SIDE, SIDE, owned, LANE), jnp.float32),
            pltpu.SemaphoreType.DMA((SIDE,)),
        ],
    )(where, index, *sources)


def sketch_kernel(where_ref, mine_zero, mine_one, sibling_zero, sibling_one, out_ref):
    core = where_ref[0]
    for j in range(SIDE):
        mine = jnp.where(core == 0, mine_zero[j], mine_one[j])
        theirs = jnp.where(core == 0, sibling_zero[j], sibling_one[j])
        out_ref[:, pl.ds(2 * j * LANE, LANE)] = jnp.where(core == 0, mine, theirs)
        out_ref[:, pl.ds((2 * j + 1) * LANE, LANE)] = jnp.where(core == 0, theirs, mine)


def sketch_rows(where, *operands):
    owned = operands[0].shape[1]
    width = 2 * SIDE * LANE
    return call(
        sketch_kernel,
        (1,),
        [fixed(operand.shape) for operand in operands],
        fixed((owned, width)),
        f32(owned, width),
        scalars=1,
    )(where, *operands)


def gram_kernel(plan, halves, where_ref, *refs):
    count = len(plan) * len(halves)
    inputs, outs = refs[:12], refs[12 : 12 + count]
    right_in, left_in, *held, out_sems = refs[12 + count :]
    core, first, second, me = (where_ref[i] for i in range(4))
    owned = right_in.shape[0] // 2
    blocks = [(number, block) for number, entries in enumerate(plan) for block in entries]

    used = [j for half in halves for j in range(CUTS[half] // 256, CUTS[half + 1] // 256)]
    for chunk in range(2):
        mine, sibling = inputs[6 * chunk], inputs[6 * chunk + 1]
        rows = pl.ds(chunk * owned, owned)
        for j in used:
            zero = 2 * j * LANE - CUTS[halves[0]]
            for side, source in enumerate((mine, sibling)):
                lanes = pl.multiple_of(zero + LANE * jnp.where(side == 0, core, 1 - core), LANE)
                right_in[rows, pl.ds(lanes, LANE)] = source[j]

    def gather(slot, k, m):
        column = jnp.where(core == 0, second ^ m, first ^ k)
        j = jnp.where(core == 0, first ^ k, second ^ m)
        distance = lax.rem(me + SIDE - column, SIDE)
        cases = [(distance == 0, 0, j), (distance == 1, 2, j), (distance == 3, 3, j)]
        cases.append(((distance == 2) & (j < 2), 4, jnp.minimum(j, 1)))
        cases.append(((distance == 2) & (j >= 2), 5, jnp.maximum(j, 2) - 2))
        for chosen, which, at in cases:

            @pl.when(chosen)
            def _():
                for chunk in range(2):
                    left_in[slot, pl.ds(chunk * owned, owned), :] = inputs[6 * chunk + which][at]

    def product(a, b):
        return lax.dot_general(a, b, (((0,), (0,)), ((), ())), preferred_element_type=jnp.float32)

    right_high, right_low = split(right_in[...])
    group = 4
    copies = []
    done = [0] * len(plan)
    for base in range(0, len(blocks), group):
        for i in range(group):
            gather(base + i, *blocks[base + i][1])
        high, low = split(jnp.concatenate([left_in[base + i] for i in range(group)], axis=1))
        for offset, half in enumerate(halves):
            here = slice(CUTS[half] - CUTS[halves[0]], CUTS[half + 1] - CUTS[halves[0]])
            value = product(high, right_high[:, here]) + product(low, right_high[:, here])
            value += product(high, right_low[:, here])
            at = list(done)
            for i in range(group):
                number = blocks[base + i][0]
                slot = len(halves) * number + offset
                held[slot][at[number]] = value[i * LANE : (i + 1) * LANE]
                at[number] += 1
                if at[number] == len(plan[number]):
                    copies.append(pltpu.make_async_copy(held[slot], outs[slot], out_sems.at[slot]))
                    copies[-1].start()
        done = at
    for copy in copies:
        copy.wait()


def gram_shares(where, operands, plan, halves):
    owned = operands[0].shape[1]
    shapes = [(len(entries), LANE, CUTS[half + 1] - CUTS[half]) for entries in plan for half in halves]
    slots = sum(len(entries) for entries in plan)
    return call(
        functools.partial(gram_kernel, plan, halves),
        (),
        [pl.BlockSpec(memory_space=pltpu.SMEM)] + [pl.BlockSpec(memory_space=pltpu.VMEM)] * len(operands),
        [pl.BlockSpec(memory_space=pl.ANY)] * len(shapes),
        [f32(*shape) for shape in shapes],
        scratch=[
            pltpu.VMEM((2 * owned, sum(CUTS[half + 1] - CUTS[half] for half in halves)), jnp.float32),
            pltpu.VMEM((slots, 2 * owned, LANE), jnp.float32),
            *[pltpu.VMEM(shape, jnp.float32) for shape in shapes],
            pltpu.SemaphoreType.DMA((len(shapes),)),
        ],
        flops=3 * 2**30,
        moved=2**23,
    )(where, *operands)


def sample_index(sample_rows, z, y, core):
    groups = lax.axis_size("row")
    spread = jnp.broadcast_to(sample_rows, (groups, sample_rows.shape[0]))
    wanted = lax.all_to_all(spread, "row", 0, 0, tiled=True).reshape(-1)
    first_here, second_here = jnp.where(core == 0, y, z), jnp.where(core == 0, z, y)
    inner, outer = wanted % 1024, wanted // 1024
    outer_z, outer_y, outer_core = outer // 8, outer // 2 % 4, outer % 2
    first = jnp.where(core == 0, outer_y, outer_z)
    second = jnp.where(core == 0, outer_z, outer_y)
    both = (first & first_here) ^ (second & second_here)
    negative = (both ^ (both >> 1) ^ (outer_core & core)) & 1
    return (inner + 1024 * (first * 2 + outer_core) + 8192 * negative).astype(jnp.int32)


def shards(design, signs, sample_rows):
    owned = sample_rows.shape[0]
    myself = lax.axis_index("row")
    column = lax.axis_index("col")
    z, y, core = myself // 8, myself // 2 % 4, myself % 2
    first, second = jnp.where(core == 0, y, z), jnp.where(core == 0, z, y)
    where = jnp.stack([core, first, second, column]).astype(jnp.int32)
    total = owned * lax.axis_size("row")
    scale = float(np.float32(1.0) / np.sqrt(np.float32(total)))

    table = jnp.asarray(hadamard(256), jnp.bfloat16)
    pieces = local_transform(where, design, signs[None, :], table)
    own, theirs = pieces[:SIDE], list(pieces[SIDE:])
    sample_rows, _ = lax.optimization_barrier((sample_rows, own[0]))
    index = sample_index(sample_rows, z, y, core)
    index, theirs[0] = lax.optimization_barrier((index, theirs[0]))
    sources = [own[0]] + [hop(own[step], FIRST, step) for step in (1, 2, 3)]
    sources += [across(theirs[step], step) for step in range(SIDE)]

    gathered = []
    for chunk in range(2):
        picked = sampled_rows(where, index, sources, scale, chunk, owned)
        arrived = [hop(picked[step], SECOND, step) for step in (1, 2, 3)]
        sums = (picked[0] + arrived[0]) + (arrived[1] + arrived[2])
        mine = exchange(sums, FIRST)
        if gathered:
            mine, *_ = lax.optimization_barrier((mine, gathered[0][2], gathered[0][3]))
        right, left = around(mine, 1), around(mine, 3)
        far_a, far_b = around(right[: SIDE // 2], 1), around(left[SIDE // 2 :], 3)
        swapped, *_ = lax.optimization_barrier((mine, right, left))
        gathered.append((mine, to_sibling(swapped), right, left, far_a, far_b))

    sketch = sketch_rows(where, gathered[0][0], gathered[1][0], gathered[0][1], gathered[1][1])

    operands = gathered[0] + gathered[1]
    low, high = (0, 1), (2, 3)

    def blocks(*entries):
        return [(first, second) for first, seconds in entries for second in seconds]

    early_plan = [blocks((2, low), (1, low)), blocks((2, high), (3, high))]
    early = [gram_shares(where, operands, early_plan, (half,)) for half in range(2)]
    late = gram_shares(where, operands, [blocks((1, high)), blocks((3, low)), blocks((0, low), (0, high))], (0, 1))
    parts = []
    for half in range(2):
        to_one, to_three = early[half]
        rest_one, rest_three, here = late[half::2]
        from_one, from_three = hop(to_one, FIRST, 1), hop(to_three, FIRST, 3)
        last_one = hop(rest_one + from_three[:2], FIRST, 1)
        last_three = hop(rest_three + from_one[:2], FIRST, 3)
        sums = [here[0] + from_one[2] + last_three[0], here[1] + from_one[3] + last_three[1]]
        sums += [here[2] + from_three[2] + last_one[0], here[3] + from_three[3] + last_one[1]]
        arrived = [hop(sums[step], SECOND, step) for step in (1, 2, 3)]
        parts.append((sums[0] + arrived[0]) + (arrived[1] + arrived[2]))
    return (sketch, jnp.concatenate(parts, axis=1))


def solution(mesh):
    in_specs = (P("row", "col"), P("row"), P("row"))
    out_specs = (P("row", "col"), P("row", "col"))
    return jax.shard_map(shards, mesh=mesh, in_specs=in_specs, out_specs=out_specs, check_vma=False)
```

```python
import functools

import jax
import jax.numpy as jnp
import numpy as np
from jax import lax
from jax.experimental import pallas as pl
from jax.experimental.pallas import tpu as pltpu
from jax.sharding import PartitionSpec as P

SIDE = 4
LANE = 128
VMEM = 40 * 2**20


def place(z, y, c):
    return z * 8 + y * 2 + c


def partners(ring, step):
    pairs = []
    for z in range(SIDE):
        for y in range(SIDE):
            for c in range(2):
                along_y = c == ring
                other = (z, y ^ step) if along_y else (z ^ step, y)
                pairs.append((place(z, y, c), place(*other, c)))
    return pairs


FIRST, SECOND = 0, 1
CUTS = (0, 512, 1024)


def groups(ring):
    lines = []
    for fixed_at in range(SIDE):
        for c in range(2):
            along_y = c == ring
            lines.append([place(fixed_at, i, c) if along_y else place(i, fixed_at, c) for i in range(SIDE)])
    return lines


def exchange(value, ring):
    return lax.all_to_all(value, "row", 0, 0, tiled=True, axis_index_groups=groups(ring))


def hop(value, ring, step):
    return lax.ppermute(value, "row", partners(ring, step))


def to_sibling(value):
    return lax.ppermute(value, "row", [(i, i ^ 1) for i in range(32)])


def across(value, step):
    return lax.ppermute(value, "row", [(i ^ 1, j) for i, j in partners(FIRST, step)])


def around(value, step):
    return lax.ppermute(value, "col", [(i, (i + step) % SIDE) for i in range(SIDE)])


def hadamard(order):
    index = np.arange(order)
    both = index[:, None] & index[None, :]
    count = np.zeros((order, order), np.int64)
    for bit in range(order.bit_length() - 1):
        count += both >> bit & 1
    return 1 - 2 * (count % 2)


def split(value):
    high = value.astype(jnp.bfloat16)
    low = (value - high.astype(jnp.float32)).astype(jnp.bfloat16)
    return high, low


def butterfly(parts):
    half = len(parts) // 2
    if half == 0:
        return parts
    low, high = butterfly(parts[:half]), butterfly(parts[half:])
    return [a + b for a, b in zip(low, high)] + [a - b for a, b in zip(low, high)]


def fixed(shape):
    return pl.BlockSpec(shape, lambda *_: (0,) * len(shape))


def f32(*shape):
    return jax.ShapeDtypeStruct(shape, jnp.float32)


def call(kernel, grid, in_specs, out_specs, out_shape, scalars=0, scratch=(), flops=2**24, moved=2**23, vmem=VMEM):
    return pl.pallas_call(
        kernel,
        grid_spec=pltpu.PrefetchScalarGridSpec(
            num_scalar_prefetch=scalars,
            grid=grid,
            in_specs=in_specs,
            out_specs=out_specs,
            scratch_shapes=scratch,
        ),
        out_shape=out_shape,
        compiler_params=pltpu.CompilerParams(vmem_limit_bytes=vmem),
        cost_estimate=pl.CostEstimate(flops=flops, bytes_accessed=moved, transcendentals=0),
    )


def local_kernel(where_ref, table_ref, signs_ref, design_ref, *refs):
    outs, (taken_ref, parts_ref, held_ref, in_sems, sems) = refs[:-5], refs[-5:]
    size = table_ref.shape[0]
    count = design_ref.shape[0] // size
    arrivals = []
    for number in range(count):
        rows = pl.ds(number * size, size)
        arrivals.append(pltpu.make_async_copy(design_ref.at[rows, :], taken_ref.at[number], in_sems.at[number]))
        arrivals[-1].start()
    for number, arrival in enumerate(arrivals):
        signed_table = table_ref[...] * signs_ref[:, pl.ds(number * size, size)].astype(jnp.bfloat16)
        arrival.wait()
        high, low = split(taken_ref[number])
        part = jnp.dot(signed_table, high, preferred_element_type=jnp.float32)
        parts_ref[number] = part + jnp.dot(signed_table, low, preferred_element_type=jnp.float32)
    copies = []
    for k in range(SIDE):
        blocks = (2 * (where_ref[1] ^ k) + where_ref[0], 2 * (where_ref[2] ^ k) + 1 - where_ref[0])
        for side, block in enumerate(blocks):
            lanes = pl.ds(pl.multiple_of(block * LANE, LANE), LANE)
            parts = butterfly([parts_ref[number, :, lanes] for number in range(count)])
            for number, part in enumerate(parts):
                held_ref[k, side, pl.ds(number * size, size), :] = part
            copies.append(pltpu.make_async_copy(held_ref.at[k, side], outs[SIDE * side + k], sems.at[k, side]))
            copies[-1].start()
    for copy in copies:
        copy.wait()


def local_transform(where, design, signs, table):
    rows, width = design.shape
    size = table.shape[0]
    count = rows // size
    return call(
        local_kernel,
        (),
        [
            pl.BlockSpec(memory_space=pltpu.SMEM),
            pl.BlockSpec(memory_space=pltpu.VMEM),
            pl.BlockSpec(memory_space=pltpu.VMEM),
            pl.BlockSpec(memory_space=pl.ANY),
        ],
        [pl.BlockSpec(memory_space=pl.ANY)] * (2 * SIDE),
        [f32(rows, LANE)] * (2 * SIDE),
        scratch=[
            pltpu.VMEM((count, size, width), jnp.float32),
            pltpu.VMEM((count, size, width), jnp.float32),
            pltpu.VMEM((SIDE, 2, rows, LANE), jnp.float32),
            pltpu.SemaphoreType.DMA((count,)),
            pltpu.SemaphoreType.DMA((SIDE, 2)),
        ],
        flops=2**30,
        moved=2**23,
        vmem=60 * 2**20,
    )(where, table, signs, design)


def sample_kernel(scale, chunk, owned, where_ref, index_ref, *refs):
    sources, outs = refs[: 2 * SIDE], refs[2 * SIDE : 3 * SIDE]
    mixed_ref, picked_ref, sems = refs[3 * SIDE :]
    rows = sources[0].shape[0]
    size = 32

    @pl.loop(0, rows // size)
    def _(number):
        here = pl.ds(pl.multiple_of(number * size, size), size)
        sums, differences = [], []
        for k in range(SIDE):
            own, other = sources[k][here, :] * scale, sources[SIDE + k][here, :] * scale
            sums.append(own + other)
            differences.append(own - other)
        for core, parts in enumerate((sums, differences)):
            for outer, part in enumerate(butterfly(parts)):
                at = (outer * 2 + core) * rows + number * size
                mixed_ref[pl.ds(pl.multiple_of(at, size), size), :] = part
                mixed_ref[pl.ds(pl.multiple_of(2 * SIDE * rows + at, size), size), :] = -part

    core, second = where_ref[0], where_ref[2]
    group = 64
    copies = []
    for m in (2, 1, 3, 0):
        for k in range(SIDE):
            outer, inner = jnp.where(core == 0, second ^ m, k), jnp.where(core == 0, k, second ^ m)
            start = (outer * 8 + inner * 2 + chunk) * owned

            @pl.loop(0, owned // group)
            def _(number):
                for lane in range(group):
                    at = number * group + lane
                    picked_ref[m, k, pl.ds(at, 1), :] = mixed_ref[pl.ds(index_ref[start + at], 1), :]

        copies.append(pltpu.make_async_copy(picked_ref.at[m], outs[m], sems.at[m]))
        copies[-1].start()
    for copy in copies:
        copy.wait()


def sampled_rows(where, index, sources, scale, chunk, owned):
    rows = sources[0].shape[0]
    return call(
        functools.partial(sample_kernel, scale, chunk, owned),
        (),
        [pl.BlockSpec(memory_space=pltpu.SMEM)] * 2 + [pl.BlockSpec(memory_space=pltpu.VMEM)] * (2 * SIDE),
        [pl.BlockSpec(memory_space=pl.ANY)] * SIDE,
        [f32(SIDE, owned, LANE)] * SIDE,
        scratch=[
            pltpu.VMEM((4 * SIDE * rows, LANE), jnp.float32),
            pltpu.VMEM((SIDE, SIDE, owned, LANE), jnp.float32),
            pltpu.SemaphoreType.DMA((SIDE,)),
        ],
    )(where, index, *sources)


def sketch_kernel(where_ref, mine_zero, mine_one, sibling_zero, sibling_one, out_ref):
    core = where_ref[0]
    for j in range(SIDE):
        mine = jnp.where(core == 0, mine_zero[j], mine_one[j])
        theirs = jnp.where(core == 0, sibling_zero[j], sibling_one[j])
        out_ref[:, pl.ds(2 * j * LANE, LANE)] = jnp.where(core == 0, mine, theirs)
        out_ref[:, pl.ds((2 * j + 1) * LANE, LANE)] = jnp.where(core == 0, theirs, mine)


def sketch_rows(where, *operands):
    owned = operands[0].shape[1]
    width = 2 * SIDE * LANE
    return call(
        sketch_kernel,
        (1,),
        [fixed(operand.shape) for operand in operands],
        fixed((owned, width)),
        f32(owned, width),
        scalars=1,
    )(where, *operands)


def gram_kernel(plan, halves, where_ref, *refs):
    count = len(plan) * len(halves)
    inputs, outs = refs[:12], refs[12 : 12 + count]
    right_in, left_in, *held, out_sems = refs[12 + count :]
    core, first, second, me = (where_ref[i] for i in range(4))
    owned = right_in.shape[0] // 2
    blocks = [(number, block) for number, entries in enumerate(plan) for block in entries]

    used = [j for half in halves for j in range(CUTS[half] // 256, CUTS[half + 1] // 256)]
    for chunk in range(2):
        mine, sibling = inputs[6 * chunk], inputs[6 * chunk + 1]
        rows = pl.ds(chunk * owned, owned)
        for j in used:
            zero = 2 * j * LANE - CUTS[halves[0]]
            for side, source in enumerate((mine, sibling)):
                lanes = pl.multiple_of(zero + LANE * jnp.where(side == 0, core, 1 - core), LANE)
                right_in[rows, pl.ds(lanes, LANE)] = source[j]

    def gather(slot, k, m):
        column = jnp.where(core == 0, second ^ m, first ^ k)
        j = jnp.where(core == 0, first ^ k, second ^ m)
        distance = lax.rem(me + SIDE - column, SIDE)
        cases = [(distance == 0, 0, j), (distance == 1, 2, j), (distance == 3, 3, j)]
        cases.append(((distance == 2) & (j < 2), 4, jnp.minimum(j, 1)))
        cases.append(((distance == 2) & (j >= 2), 5, jnp.maximum(j, 2) - 2))
        for chosen, which, at in cases:

            @pl.when(chosen)
            def _():
                for chunk in range(2):
                    left_in[slot, pl.ds(chunk * owned, owned), :] = inputs[6 * chunk + which][at]

    def product(a, b):
        return lax.dot_general(a, b, (((0,), (0,)), ((), ())), preferred_element_type=jnp.float32)

    right_high, right_low = split(right_in[...])
    group = 4
    copies = []
    done = [0] * len(plan)
    for base in range(0, len(blocks), group):
        for i in range(group):
            gather(base + i, *blocks[base + i][1])
        high, low = split(jnp.concatenate([left_in[base + i] for i in range(group)], axis=1))
        for offset, half in enumerate(halves):
            here = slice(CUTS[half] - CUTS[halves[0]], CUTS[half + 1] - CUTS[halves[0]])
            value = product(high, right_high[:, here]) + product(low, right_high[:, here])
            value += product(high, right_low[:, here])
            at = list(done)
            for i in range(group):
                number = blocks[base + i][0]
                slot = len(halves) * number + offset
                held[slot][at[number]] = value[i * LANE : (i + 1) * LANE]
                at[number] += 1
                if at[number] == len(plan[number]):
                    copies.append(pltpu.make_async_copy(held[slot], outs[slot], out_sems.at[slot]))
                    copies[-1].start()
        done = at
    for copy in copies:
        copy.wait()


def gram_shares(where, operands, plan, halves):
    owned = operands[0].shape[1]
    shapes = [(len(entries), LANE, CUTS[half + 1] - CUTS[half]) for entries in plan for half in halves]
    slots = sum(len(entries) for entries in plan)
    return call(
        functools.partial(gram_kernel, plan, halves),
        (),
        [pl.BlockSpec(memory_space=pltpu.SMEM)] + [pl.BlockSpec(memory_space=pltpu.VMEM)] * len(operands),
        [pl.BlockSpec(memory_space=pl.ANY)] * len(shapes),
        [f32(*shape) for shape in shapes],
        scratch=[
            pltpu.VMEM((2 * owned, sum(CUTS[half + 1] - CUTS[half] for half in halves)), jnp.float32),
            pltpu.VMEM((slots, 2 * owned, LANE), jnp.float32),
            *[pltpu.VMEM(shape, jnp.float32) for shape in shapes],
            pltpu.SemaphoreType.DMA((len(shapes),)),
        ],
        flops=3 * 2**30,
        moved=2**23,
    )(where, *operands)


def sample_index(sample_rows, z, y, core):
    groups = lax.axis_size("row")
    spread = jnp.broadcast_to(sample_rows, (groups, sample_rows.shape[0]))
    wanted = lax.all_to_all(spread, "row", 0, 0, tiled=True).reshape(-1)
    first_here, second_here = jnp.where(core == 0, y, z), jnp.where(core == 0, z, y)
    inner, outer = wanted % 1024, wanted // 1024
    outer_z, outer_y, outer_core = outer // 8, outer // 2 % 4, outer % 2
    first = jnp.where(core == 0, outer_y, outer_z)
    second = jnp.where(core == 0, outer_z, outer_y)
    both = (first & first_here) ^ (second & second_here)
    negative = (both ^ (both >> 1) ^ (outer_core & core)) & 1
    return (inner + 1024 * (first * 2 + outer_core) + 8192 * negative).astype(jnp.int32)


def shards(design, signs, sample_rows):
    owned = sample_rows.shape[0]
    myself = lax.axis_index("row")
    column = lax.axis_index("col")
    z, y, core = myself // 8, myself // 2 % 4, myself % 2
    first, second = jnp.where(core == 0, y, z), jnp.where(core == 0, z, y)
    where = jnp.stack([core, first, second, column]).astype(jnp.int32)
    total = owned * lax.axis_size("row")
    scale = float(np.float32(1.0) / np.sqrt(np.float32(total)))

    table = jnp.asarray(hadamard(256), jnp.bfloat16)
    pieces = local_transform(where, design, signs[None, :], table)
    own, theirs = pieces[:SIDE], list(pieces[SIDE:])
    sample_rows, _ = lax.optimization_barrier((sample_rows, own[0]))
    index = sample_index(sample_rows, z, y, core)
    index, theirs[0] = lax.optimization_barrier((index, theirs[0]))
    sources = [own[0]] + [hop(own[step], FIRST, step) for step in (1, 2, 3)]
    sources += [across(theirs[step], step) for step in range(SIDE)]

    gathered = []
    for chunk in range(2):
        picked = sampled_rows(where, index, sources, scale, chunk, owned)
        arrived = [hop(picked[step], SECOND, step) for step in (1, 2, 3)]
        sums = (picked[0] + arrived[0]) + (arrived[1] + arrived[2])
        mine = exchange(sums, FIRST)
        if gathered:
            mine, *_ = lax.optimization_barrier((mine, *gathered[0][1:4]))
        right, left = around(mine, 1), around(mine, 3)
        swapped, onward, back = mine, right, left
        if gathered:
            swapped, onward, back, *_ = lax.optimization_barrier((mine, right, left, *gathered[0][4:]))
        far_a, far_b = around(onward[: SIDE // 2], 1), around(back[SIDE // 2 :], 3)
        gathered.append((mine, to_sibling(swapped), right, left, far_a, far_b))

    sketch = sketch_rows(where, gathered[0][0], gathered[1][0], gathered[0][1], gathered[1][1])

    operands = gathered[0] + gathered[1]
    low, high = (0, 1), (2, 3)

    def blocks(*entries):
        return [(first, second) for first, seconds in entries for second in seconds]

    early_plan = [blocks((2, low), (1, low)), blocks((2, high), (3, high))]
    early = [gram_shares(where, operands, early_plan, (half,)) for half in range(2)]
    late = gram_shares(where, operands, [blocks((1, high)), blocks((3, low)), blocks((0, low), (0, high))], (0, 1))
    parts = []
    for half in range(2):
        to_one, to_three = early[half]
        rest_one, rest_three, here = late[half::2]
        from_one, from_three = hop(to_one, FIRST, 1), hop(to_three, FIRST, 3)
        last_one = hop(rest_one + from_three[:2], FIRST, 1)
        last_three = hop(rest_three + from_one[:2], FIRST, 3)
        sums = [here[0] + from_one[2] + last_three[0], here[1] + from_one[3] + last_three[1]]
        sums += [here[2] + from_three[2] + last_one[0], here[3] + from_three[3] + last_one[1]]
        arrived = [hop(sums[step], SECOND, step) for step in (1, 2, 3)]
        parts.append((sums[0] + arrived[0]) + (arrived[1] + arrived[2]))
    return (sketch, jnp.concatenate(parts, axis=1))


def solution(mesh):
    in_specs = (P("row", "col"), P("row"), P("row"))
    out_specs = (P("row", "col"), P("row", "col"))
    return jax.shard_map(shards, mesh=mesh, in_specs=in_specs, out_specs=out_specs, check_vma=False)
```

```python
import functools

import jax
import jax.numpy as jnp
import numpy as np
from jax import lax
from jax.experimental import pallas as pl
from jax.experimental.pallas import tpu as pltpu
from jax.sharding import PartitionSpec as P

SIDE = 4
LANE = 128
VMEM = 40 * 2**20


def place(z, y, c):
    return z * 8 + y * 2 + c


def partners(ring, step):
    pairs = []
    for z in range(SIDE):
        for y in range(SIDE):
            for c in range(2):
                along_y = c == ring
                other = (z, y ^ step) if along_y else (z ^ step, y)
                pairs.append((place(z, y, c), place(*other, c)))
    return pairs


FIRST, SECOND = 0, 1
CUTS = (0, 512, 1024)


def ring_places(index):
    z, y, core = index // 8, index // 2 % 4, index % 2
    return core, jnp.where(core == 0, y, z), jnp.where(core == 0, z, y)


def groups(ring):
    lines = []
    for fixed_at in range(SIDE):
        for c in range(2):
            along_y = c == ring
            lines.append([place(fixed_at, i, c) if along_y else place(i, fixed_at, c) for i in range(SIDE)])
    return lines


def exchange(value, ring):
    return lax.all_to_all(value, "row", 0, 0, tiled=True, axis_index_groups=groups(ring))


def hop(value, ring, step):
    return lax.ppermute(value, "row", partners(ring, step))


def to_sibling(value):
    return lax.ppermute(value, "row", [(i, i ^ 1) for i in range(32)])


def across(value, step):
    return lax.ppermute(value, "row", [(i ^ 1, j) for i, j in partners(FIRST, step)])


def around(value, step):
    return lax.ppermute(value, "col", [(i, (i + step) % SIDE) for i in range(SIDE)])


def hadamard(order):
    index = np.arange(order)
    both = index[:, None] & index[None, :]
    count = np.zeros((order, order), np.int64)
    for bit in range(order.bit_length() - 1):
        count += both >> bit & 1
    return 1 - 2 * (count % 2)


def split(value):
    high = value.astype(jnp.bfloat16)
    low = (value - high.astype(jnp.float32)).astype(jnp.bfloat16)
    return high, low


def butterfly(parts):
    half = len(parts) // 2
    if half == 0:
        return parts
    low, high = butterfly(parts[:half]), butterfly(parts[half:])
    return [a + b for a, b in zip(low, high)] + [a - b for a, b in zip(low, high)]


def fixed(shape):
    return pl.BlockSpec(shape, lambda *_: (0,) * len(shape))


def f32(*shape):
    return jax.ShapeDtypeStruct(shape, jnp.float32)


def call(kernel, grid, in_specs, out_specs, out_shape, scalars=0, scratch=(), flops=2**24, moved=2**23, vmem=VMEM):
    return pl.pallas_call(
        kernel,
        grid_spec=pltpu.PrefetchScalarGridSpec(
            num_scalar_prefetch=scalars,
            grid=grid,
            in_specs=in_specs,
            out_specs=out_specs,
            scratch_shapes=scratch,
        ),
        out_shape=out_shape,
        compiler_params=pltpu.CompilerParams(vmem_limit_bytes=vmem),
        cost_estimate=pl.CostEstimate(flops=flops, bytes_accessed=moved, transcendentals=0),
    )


def local_kernel(table_ref, signs_ref, design_ref, *refs):
    core, first, second = ring_places(lax.axis_index("row"))
    outs, (taken_ref, parts_ref, held_ref, in_sems, sems) = refs[:-5], refs[-5:]
    size = table_ref.shape[0]
    count = design_ref.shape[0] // size
    arrivals = []
    for number in range(count):
        rows = pl.ds(number * size, size)
        arrivals.append(pltpu.make_async_copy(design_ref.at[rows, :], taken_ref.at[number], in_sems.at[number]))
        arrivals[-1].start()
    for number, arrival in enumerate(arrivals):
        signed_table = table_ref[...] * signs_ref[:, pl.ds(number * size, size)].astype(jnp.bfloat16)
        arrival.wait()
        high, low = split(taken_ref[number])
        part = jnp.dot(signed_table, high, preferred_element_type=jnp.float32)
        parts_ref[number] = part + jnp.dot(signed_table, low, preferred_element_type=jnp.float32)
    copies = []
    for k in range(SIDE):
        blocks = (2 * (first ^ k) + core, 2 * (second ^ k) + 1 - core)
        for side, block in enumerate(blocks):
            lanes = pl.ds(pl.multiple_of(block * LANE, LANE), LANE)
            parts = butterfly([parts_ref[number, :, lanes] for number in range(count)])
            for number, part in enumerate(parts):
                held_ref[k, side, pl.ds(number * size, size), :] = part
            copies.append(pltpu.make_async_copy(held_ref.at[k, side], outs[SIDE * side + k], sems.at[k, side]))
            copies[-1].start()
    for copy in copies:
        copy.wait()


def local_transform(design, signs, table):
    rows, width = design.shape
    size = table.shape[0]
    count = rows // size
    return call(
        local_kernel,
        (),
        [
            pl.BlockSpec(memory_space=pltpu.VMEM),
            pl.BlockSpec(memory_space=pltpu.VMEM),
            pl.BlockSpec(memory_space=pl.ANY),
        ],
        [pl.BlockSpec(memory_space=pl.ANY)] * (2 * SIDE),
        [f32(rows, LANE)] * (2 * SIDE),
        scratch=[
            pltpu.VMEM((count, size, width), jnp.float32),
            pltpu.VMEM((count, size, width), jnp.float32),
            pltpu.VMEM((SIDE, 2, rows, LANE), jnp.float32),
            pltpu.SemaphoreType.DMA((count,)),
            pltpu.SemaphoreType.DMA((SIDE, 2)),
        ],
        flops=2**30,
        moved=2**23,
        vmem=60 * 2**20,
    )(table, signs, design)


def sample_kernel(scale, chunk, owned, where_ref, index_ref, *refs):
    sources, outs = refs[: 2 * SIDE], refs[2 * SIDE : 3 * SIDE]
    mixed_ref, picked_ref, sems = refs[3 * SIDE :]
    rows = sources[0].shape[0]
    size = 32

    @pl.loop(0, rows // size)
    def _(number):
        here = pl.ds(pl.multiple_of(number * size, size), size)
        sums, differences = [], []
        for k in range(SIDE):
            own, other = sources[k][here, :] * scale, sources[SIDE + k][here, :] * scale
            sums.append(own + other)
            differences.append(own - other)
        for core, parts in enumerate((sums, differences)):
            for outer, part in enumerate(butterfly(parts)):
                at = (outer * 2 + core) * rows + number * size
                mixed_ref[pl.ds(pl.multiple_of(at, size), size), :] = part
                mixed_ref[pl.ds(pl.multiple_of(2 * SIDE * rows + at, size), size), :] = -part

    core, second = where_ref[0], where_ref[2]
    group = 64
    copies = []
    for m in (2, 1, 3, 0):
        for k in range(SIDE):
            outer, inner = jnp.where(core == 0, second ^ m, k), jnp.where(core == 0, k, second ^ m)
            start = (outer * 8 + inner * 2 + chunk) * owned

            @pl.loop(0, owned // group)
            def _(number):
                for lane in range(group):
                    at = number * group + lane
                    picked_ref[m, k, pl.ds(at, 1), :] = mixed_ref[pl.ds(index_ref[start + at], 1), :]

        copies.append(pltpu.make_async_copy(picked_ref.at[m], outs[m], sems.at[m]))
        copies[-1].start()
    for copy in copies:
        copy.wait()


def sampled_rows(where, index, sources, scale, chunk, owned):
    rows = sources[0].shape[0]
    return call(
        functools.partial(sample_kernel, scale, chunk, owned),
        (),
        [pl.BlockSpec(memory_space=pltpu.SMEM)] * 2 + [pl.BlockSpec(memory_space=pltpu.VMEM)] * (2 * SIDE),
        [pl.BlockSpec(memory_space=pl.ANY)] * SIDE,
        [f32(SIDE, owned, LANE)] * SIDE,
        scratch=[
            pltpu.VMEM((4 * SIDE * rows, LANE), jnp.float32),
            pltpu.VMEM((SIDE, SIDE, owned, LANE), jnp.float32),
            pltpu.SemaphoreType.DMA((SIDE,)),
        ],
    )(where, index, *sources)


def sketch_kernel(where_ref, mine_zero, mine_one, sibling_zero, sibling_one, out_ref):
    core = where_ref[0]
    for j in range(SIDE):
        mine = jnp.where(core == 0, mine_zero[j], mine_one[j])
        theirs = jnp.where(core == 0, sibling_zero[j], sibling_one[j])
        out_ref[:, pl.ds(2 * j * LANE, LANE)] = jnp.where(core == 0, mine, theirs)
        out_ref[:, pl.ds((2 * j + 1) * LANE, LANE)] = jnp.where(core == 0, theirs, mine)


def sketch_rows(where, *operands):
    owned = operands[0].shape[1]
    width = 2 * SIDE * LANE
    return call(
        sketch_kernel,
        (1,),
        [fixed(operand.shape) for operand in operands],
        fixed((owned, width)),
        f32(owned, width),
        scalars=1,
    )(where, *operands)


def gram_kernel(plan, halves, where_ref, *refs):
    count = len(plan) * len(halves)
    inputs, outs = refs[:12], refs[12 : 12 + count]
    right_in, left_in, *held, out_sems = refs[12 + count :]
    core, first, second, me = (where_ref[i] for i in range(4))
    owned = right_in.shape[0] // 2
    blocks = [(number, block) for number, entries in enumerate(plan) for block in entries]

    used = [j for half in halves for j in range(CUTS[half] // 256, CUTS[half + 1] // 256)]
    for chunk in range(2):
        mine, sibling = inputs[6 * chunk], inputs[6 * chunk + 1]
        rows = pl.ds(chunk * owned, owned)
        for j in used:
            zero = 2 * j * LANE - CUTS[halves[0]]
            for side, source in enumerate((mine, sibling)):
                lanes = pl.multiple_of(zero + LANE * jnp.where(side == 0, core, 1 - core), LANE)
                right_in[rows, pl.ds(lanes, LANE)] = source[j]

    def gather(slot, k, m):
        column = jnp.where(core == 0, second ^ m, first ^ k)
        j = jnp.where(core == 0, first ^ k, second ^ m)
        distance = lax.rem(me + SIDE - column, SIDE)
        cases = [(distance == 0, 0, j), (distance == 1, 2, j), (distance == 3, 3, j)]
        cases.append(((distance == 2) & (j < 2), 4, jnp.minimum(j, 1)))
        cases.append(((distance == 2) & (j >= 2), 5, jnp.maximum(j, 2) - 2))
        for chosen, which, at in cases:

            @pl.when(chosen)
            def _():
                for chunk in range(2):
                    left_in[slot, pl.ds(chunk * owned, owned), :] = inputs[6 * chunk + which][at]

    def product(a, b):
        return lax.dot_general(a, b, (((0,), (0,)), ((), ())), preferred_element_type=jnp.float32)

    right_high, right_low = split(right_in[...])
    group = 4
    copies = []
    done = [0] * len(plan)
    for base in range(0, len(blocks), group):
        for i in range(group):
            gather(base + i, *blocks[base + i][1])
        high, low = split(jnp.concatenate([left_in[base + i] for i in range(group)], axis=1))
        for offset, half in enumerate(halves):
            here = slice(CUTS[half] - CUTS[halves[0]], CUTS[half + 1] - CUTS[halves[0]])
            value = product(high, right_high[:, here]) + product(low, right_high[:, here])
            value += product(high, right_low[:, here])
            at = list(done)
            for i in range(group):
                number = blocks[base + i][0]
                slot = len(halves) * number + offset
                held[slot][at[number]] = value[i * LANE : (i + 1) * LANE]
                at[number] += 1
                if at[number] == len(plan[number]):
                    copies.append(pltpu.make_async_copy(held[slot], outs[slot], out_sems.at[slot]))
                    copies[-1].start()
        done = at
    for copy in copies:
        copy.wait()


def gram_shares(where, operands, plan, halves):
    owned = operands[0].shape[1]
    shapes = [(len(entries), LANE, CUTS[half + 1] - CUTS[half]) for entries in plan for half in halves]
    slots = sum(len(entries) for entries in plan)
    return call(
        functools.partial(gram_kernel, plan, halves),
        (),
        [pl.BlockSpec(memory_space=pltpu.SMEM)] + [pl.BlockSpec(memory_space=pltpu.VMEM)] * len(operands),
        [pl.BlockSpec(memory_space=pl.ANY)] * len(shapes),
        [f32(*shape) for shape in shapes],
        scratch=[
            pltpu.VMEM((2 * owned, sum(CUTS[half + 1] - CUTS[half] for half in halves)), jnp.float32),
            pltpu.VMEM((slots, 2 * owned, LANE), jnp.float32),
            *[pltpu.VMEM(shape, jnp.float32) for shape in shapes],
            pltpu.SemaphoreType.DMA((len(shapes),)),
        ],
        flops=3 * 2**30,
        moved=2**23,
    )(where, *operands)


def sample_index(sample_rows, z, y, core):
    groups = lax.axis_size("row")
    spread = jnp.broadcast_to(sample_rows, (groups, sample_rows.shape[0]))
    wanted = lax.all_to_all(spread, "row", 0, 0, tiled=True).reshape(-1)
    first_here, second_here = jnp.where(core == 0, y, z), jnp.where(core == 0, z, y)
    inner, outer = wanted % 1024, wanted // 1024
    outer_z, outer_y, outer_core = outer // 8, outer // 2 % 4, outer % 2
    first = jnp.where(core == 0, outer_y, outer_z)
    second = jnp.where(core == 0, outer_z, outer_y)
    both = (first & first_here) ^ (second & second_here)
    negative = (both ^ (both >> 1) ^ (outer_core & core)) & 1
    return (inner + 1024 * (first * 2 + outer_core) + 8192 * negative).astype(jnp.int32)


def shards(design, signs, sample_rows):
    owned = sample_rows.shape[0]
    myself = lax.axis_index("row")
    column = lax.axis_index("col")
    z, y, core = myself // 8, myself // 2 % 4, myself % 2
    first, second = jnp.where(core == 0, y, z), jnp.where(core == 0, z, y)
    where = jnp.stack([core, first, second, column]).astype(jnp.int32)
    total = owned * lax.axis_size("row")
    scale = float(np.float32(1.0) / np.sqrt(np.float32(total)))

    table = jnp.asarray(hadamard(256), jnp.bfloat16)
    pieces = local_transform(design, signs[None, :], table)
    own, theirs = pieces[:SIDE], list(pieces[SIDE:])
    sample_rows, _ = lax.optimization_barrier((sample_rows, own[0]))
    index = sample_index(sample_rows, z, y, core)
    index, theirs[0] = lax.optimization_barrier((index, theirs[0]))
    sources = [own[0]] + [hop(own[step], FIRST, step) for step in (1, 2, 3)]
    sources += [across(theirs[step], step) for step in range(SIDE)]

    gathered = []
    for chunk in range(2):
        picked = sampled_rows(where, index, sources, scale, chunk, owned)
        arrived = [hop(picked[step], SECOND, step) for step in (1, 2, 3)]
        sums = (picked[0] + arrived[0]) + (arrived[1] + arrived[2])
        mine = exchange(sums, FIRST)
        if gathered:
            mine, *_ = lax.optimization_barrier((mine, *gathered[0][1:4]))
        right, left = around(mine, 1), around(mine, 3)
        swapped, onward, back = mine, right, left
        if gathered:
            swapped, onward, back, *_ = lax.optimization_barrier((mine, right, left, *gathered[0][4:]))
        far_a, far_b = around(onward[: SIDE // 2], 1), around(back[SIDE // 2 :], 3)
        gathered.append((mine, to_sibling(swapped), right, left, far_a, far_b))

    sketch = sketch_rows(where, gathered[0][0], gathered[1][0], gathered[0][1], gathered[1][1])

    operands = gathered[0] + gathered[1]
    low, high = (0, 1), (2, 3)

    def blocks(*entries):
        return [(first, second) for first, seconds in entries for second in seconds]

    early_plan = [blocks((2, low), (1, low)), blocks((2, high), (3, high))]
    early = [gram_shares(where, operands, early_plan, (half,)) for half in range(2)]
    late = gram_shares(where, operands, [blocks((1, high)), blocks((3, low)), blocks((0, low), (0, high))], (0, 1))
    parts = []
    for half in range(2):
        to_one, to_three = early[half]
        rest_one, rest_three, here = late[half::2]
        from_one, from_three = hop(to_one, FIRST, 1), hop(to_three, FIRST, 3)
        last_one = hop(rest_one + from_three[:2], FIRST, 1)
        last_three = hop(rest_three + from_one[:2], FIRST, 3)
        sums = [here[0] + from_one[2] + last_three[0], here[1] + from_one[3] + last_three[1]]
        sums += [here[2] + from_three[2] + last_one[0], here[3] + from_three[3] + last_one[1]]
        arrived = [hop(sums[step], SECOND, step) for step in (1, 2, 3)]
        parts.append((sums[0] + arrived[0]) + (arrived[1] + arrived[2]))
    return (sketch, jnp.concatenate(parts, axis=1))


def solution(mesh):
    in_specs = (P("row", "col"), P("row"), P("row"))
    out_specs = (P("row", "col"), P("row", "col"))
    return jax.shard_map(shards, mesh=mesh, in_specs=in_specs, out_specs=out_specs, check_vma=False)
```

```python
import functools

import jax
import jax.numpy as jnp
import numpy as np
from jax import lax
from jax.experimental import pallas as pl
from jax.experimental.pallas import tpu as pltpu
from jax.sharding import PartitionSpec as P

SIDE = 4
LANE = 128
VMEM = 28 * 2**20


def place(z, y, c):
    return z * 8 + y * 2 + c


def partners(ring, step):
    pairs = []
    for z in range(SIDE):
        for y in range(SIDE):
            for c in range(2):
                along_y = c == ring
                other = (z, y ^ step) if along_y else (z ^ step, y)
                pairs.append((place(z, y, c), place(*other, c)))
    return pairs


FIRST, SECOND = 0, 1
CUTS = (0, 512, 1024)


def ring_places(index):
    z, y, core = index // 8, index // 2 % 4, index % 2
    return core, jnp.where(core == 0, y, z), jnp.where(core == 0, z, y)


def groups(ring):
    lines = []
    for fixed_at in range(SIDE):
        for c in range(2):
            along_y = c == ring
            lines.append([place(fixed_at, i, c) if along_y else place(i, fixed_at, c) for i in range(SIDE)])
    return lines


def exchange(value, ring):
    return lax.all_to_all(value, "row", 0, 0, tiled=True, axis_index_groups=groups(ring))


def hop(value, ring, step):
    return lax.ppermute(value, "row", partners(ring, step))


def to_sibling(value):
    return lax.ppermute(value, "row", [(i, i ^ 1) for i in range(32)])


def across(value, step):
    return lax.ppermute(value, "row", [(i ^ 1, j) for i, j in partners(FIRST, step)])


def around(value, step):
    return lax.ppermute(value, "col", [(i, (i + step) % SIDE) for i in range(SIDE)])


def hadamard(order):
    index = np.arange(order)
    both = index[:, None] & index[None, :]
    count = np.zeros((order, order), np.int64)
    for bit in range(order.bit_length() - 1):
        count += both >> bit & 1
    return 1 - 2 * (count % 2)


def split(value):
    high = value.astype(jnp.bfloat16)
    low = (value - high.astype(jnp.float32)).astype(jnp.bfloat16)
    return high, low


def butterfly(parts):
    half = len(parts) // 2
    if half == 0:
        return parts
    low, high = butterfly(parts[:half]), butterfly(parts[half:])
    return [a + b for a, b in zip(low, high)] + [a - b for a, b in zip(low, high)]


def fixed(shape):
    return pl.BlockSpec(shape, lambda *_: (0,) * len(shape))


def f32(*shape):
    return jax.ShapeDtypeStruct(shape, jnp.float32)


def call(kernel, grid, in_specs, out_specs, out_shape, scalars=0, scratch=(), flops=2**24, moved=2**23, vmem=VMEM):
    return pl.pallas_call(
        kernel,
        grid_spec=pltpu.PrefetchScalarGridSpec(
            num_scalar_prefetch=scalars,
            grid=grid,
            in_specs=in_specs,
            out_specs=out_specs,
            scratch_shapes=scratch,
        ),
        out_shape=out_shape,
        compiler_params=pltpu.CompilerParams(vmem_limit_bytes=vmem),
        cost_estimate=pl.CostEstimate(flops=flops, bytes_accessed=moved, transcendentals=0),
    )


def local_kernel(table_ref, signs_ref, design_ref, *refs):
    core, first, second = ring_places(lax.axis_index("row"))
    outs, (taken_ref, parts_ref, held_ref, in_sems, sems) = refs[:-5], refs[-5:]
    size = table_ref.shape[0]
    count = design_ref.shape[0] // size
    arrivals = []
    for number in range(count):
        rows = pl.ds(number * size, size)
        arrivals.append(pltpu.make_async_copy(design_ref.at[rows, :], taken_ref.at[number], in_sems.at[number]))
        arrivals[-1].start()
    for number, arrival in enumerate(arrivals):
        signed_table = table_ref[...] * signs_ref[:, pl.ds(number * size, size)].astype(jnp.bfloat16)
        arrival.wait()
        high, low = split(taken_ref[number])
        part = jnp.dot(signed_table, high, preferred_element_type=jnp.float32)
        parts_ref[number] = part + jnp.dot(signed_table, low, preferred_element_type=jnp.float32)
    copies = []
    for k in range(SIDE):
        blocks = (2 * (first ^ k) + core, 2 * (second ^ k) + 1 - core)
        for side, block in enumerate(blocks):
            lanes = pl.ds(pl.multiple_of(block * LANE, LANE), LANE)
            parts = butterfly([parts_ref[number, :, lanes] for number in range(count)])
            for number, part in enumerate(parts):
                held_ref[k, side, pl.ds(number * size, size), :] = part
            copies.append(pltpu.make_async_copy(held_ref.at[k, side], outs[SIDE * side + k], sems.at[k, side]))
            copies[-1].start()
    for copy in copies:
        copy.wait()


def local_transform(design, signs, table):
    rows, width = design.shape
    size = table.shape[0]
    count = rows // size
    return call(
        local_kernel,
        (),
        [
            pl.BlockSpec(memory_space=pltpu.VMEM),
            pl.BlockSpec(memory_space=pltpu.VMEM),
            pl.BlockSpec(memory_space=pl.ANY),
        ],
        [pl.BlockSpec(memory_space=pl.ANY)] * (2 * SIDE),
        [f32(rows, LANE)] * (2 * SIDE),
        scratch=[
            pltpu.VMEM((count, size, width), jnp.float32),
            pltpu.VMEM((count, size, width), jnp.float32),
            pltpu.VMEM((SIDE, 2, rows, LANE), jnp.float32),
            pltpu.SemaphoreType.DMA((count,)),
            pltpu.SemaphoreType.DMA((SIDE, 2)),
        ],
        flops=2**30,
        moved=2**23,
        vmem=60 * 2**20,
    )(table, signs, design)


def sample_kernel(scale, chunk, owned, where_ref, index_ref, *refs):
    sources, outs = refs[: 2 * SIDE], refs[2 * SIDE : 3 * SIDE]
    mixed_ref, picked_ref, sems = refs[3 * SIDE :]
    rows = sources[0].shape[0]
    size = 32

    @pl.loop(0, rows // size)
    def _(number):
        here = pl.ds(pl.multiple_of(number * size, size), size)
        sums, differences = [], []
        for k in range(SIDE):
            own, other = sources[k][here, :] * scale, sources[SIDE + k][here, :] * scale
            sums.append(own + other)
            differences.append(own - other)
        for core, parts in enumerate((sums, differences)):
            for outer, part in enumerate(butterfly(parts)):
                at = (outer * 2 + core) * rows + number * size
                mixed_ref[pl.ds(pl.multiple_of(at, size), size), :] = part
                mixed_ref[pl.ds(pl.multiple_of(2 * SIDE * rows + at, size), size), :] = -part

    core, second = where_ref[0], where_ref[2]
    group = 64
    copies = []
    for m in (2, 1, 3, 0):
        for k in range(SIDE):
            outer, inner = jnp.where(core == 0, second ^ m, k), jnp.where(core == 0, k, second ^ m)
            start = (outer * 8 + inner * 2 + chunk) * owned

            @pl.loop(0, owned // group)
            def _(number):
                for lane in range(group):
                    at = number * group + lane
                    picked_ref[m, k, pl.ds(at, 1), :] = mixed_ref[pl.ds(index_ref[start + at], 1), :]

        copies.append(pltpu.make_async_copy(picked_ref.at[m], outs[m], sems.at[m]))
        copies[-1].start()
    for copy in copies:
        copy.wait()


def sampled_rows(where, index, sources, scale, chunk, owned):
    rows = sources[0].shape[0]
    return call(
        functools.partial(sample_kernel, scale, chunk, owned),
        (),
        [pl.BlockSpec(memory_space=pltpu.SMEM)] * 2 + [pl.BlockSpec(memory_space=pltpu.VMEM)] * (2 * SIDE),
        [pl.BlockSpec(memory_space=pl.ANY)] * SIDE,
        [f32(SIDE, owned, LANE)] * SIDE,
        scratch=[
            pltpu.VMEM((4 * SIDE * rows, LANE), jnp.float32),
            pltpu.VMEM((SIDE, SIDE, owned, LANE), jnp.float32),
            pltpu.SemaphoreType.DMA((SIDE,)),
        ],
    )(where, index, *sources)


def sketch_kernel(where_ref, mine_zero, mine_one, sibling_zero, sibling_one, out_ref):
    core = where_ref[0]
    for j in range(SIDE):
        mine = jnp.where(core == 0, mine_zero[j], mine_one[j])
        theirs = jnp.where(core == 0, sibling_zero[j], sibling_one[j])
        out_ref[:, pl.ds(2 * j * LANE, LANE)] = jnp.where(core == 0, mine, theirs)
        out_ref[:, pl.ds((2 * j + 1) * LANE, LANE)] = jnp.where(core == 0, theirs, mine)


def sketch_rows(where, *operands):
    owned = operands[0].shape[1]
    width = 2 * SIDE * LANE
    return call(
        sketch_kernel,
        (1,),
        [fixed(operand.shape) for operand in operands],
        fixed((owned, width)),
        f32(owned, width),
        scalars=1,
    )(where, *operands)


def gram_kernel(plan, halves, where_ref, *refs):
    count = len(plan) * len(halves)
    inputs, outs = refs[:12], refs[12 : 12 + count]
    right_in, left_in, *held, out_sems = refs[12 + count :]
    core, first, second, me = (where_ref[i] for i in range(4))
    owned = right_in.shape[0] // 2
    blocks = [(number, block) for number, entries in enumerate(plan) for block in entries]

    used = [j for half in halves for j in range(CUTS[half] // 256, CUTS[half + 1] // 256)]
    for chunk in range(2):
        mine, sibling = inputs[6 * chunk], inputs[6 * chunk + 1]
        rows = pl.ds(chunk * owned, owned)
        for j in used:
            zero = 2 * j * LANE - CUTS[halves[0]]
            for side, source in enumerate((mine, sibling)):
                lanes = pl.multiple_of(zero + LANE * jnp.where(side == 0, core, 1 - core), LANE)
                right_in[rows, pl.ds(lanes, LANE)] = source[j]

    def gather(slot, k, m):
        column = jnp.where(core == 0, second ^ m, first ^ k)
        j = jnp.where(core == 0, first ^ k, second ^ m)
        distance = lax.rem(me + SIDE - column, SIDE)
        cases = [(distance == 0, 0, j), (distance == 1, 2, j), (distance == 3, 3, j)]
        cases.append(((distance == 2) & (j < 2), 4, jnp.minimum(j, 1)))
        cases.append(((distance == 2) & (j >= 2), 5, jnp.maximum(j, 2) - 2))
        for chosen, which, at in cases:

            @pl.when(chosen)
            def _():
                for chunk in range(2):
                    left_in[slot, pl.ds(chunk * owned, owned), :] = inputs[6 * chunk + which][at]

    def product(a, b):
        return lax.dot_general(a, b, (((0,), (0,)), ((), ())), preferred_element_type=jnp.float32)

    right_high, right_low = split(right_in[...])
    group = 4
    copies = []
    done = [0] * len(plan)
    for base in range(0, len(blocks), group):
        for i in range(group):
            gather(base + i, *blocks[base + i][1])
        high, low = split(jnp.concatenate([left_in[base + i] for i in range(group)], axis=1))
        for offset, half in enumerate(halves):
            here = slice(CUTS[half] - CUTS[halves[0]], CUTS[half + 1] - CUTS[halves[0]])
            value = product(high, right_high[:, here]) + product(low, right_high[:, here])
            value += product(high, right_low[:, here])
            at = list(done)
            for i in range(group):
                number = blocks[base + i][0]
                slot = len(halves) * number + offset
                held[slot][at[number]] = value[i * LANE : (i + 1) * LANE]
                at[number] += 1
                if at[number] == len(plan[number]):
                    copies.append(pltpu.make_async_copy(held[slot], outs[slot], out_sems.at[slot]))
                    copies[-1].start()
        done = at
    for copy in copies:
        copy.wait()


def gram_shares(where, operands, plan, halves):
    owned = operands[0].shape[1]
    shapes = [(len(entries), LANE, CUTS[half + 1] - CUTS[half]) for entries in plan for half in halves]
    slots = sum(len(entries) for entries in plan)
    return call(
        functools.partial(gram_kernel, plan, halves),
        (),
        [pl.BlockSpec(memory_space=pltpu.SMEM)] + [pl.BlockSpec(memory_space=pltpu.VMEM)] * len(operands),
        [pl.BlockSpec(memory_space=pl.ANY)] * len(shapes),
        [f32(*shape) for shape in shapes],
        scratch=[
            pltpu.VMEM((2 * owned, sum(CUTS[half + 1] - CUTS[half] for half in halves)), jnp.float32),
            pltpu.VMEM((slots, 2 * owned, LANE), jnp.float32),
            *[pltpu.VMEM(shape, jnp.float32) for shape in shapes],
            pltpu.SemaphoreType.DMA((len(shapes),)),
        ],
        flops=3 * 2**30,
        moved=2**23,
    )(where, *operands)


def sample_index(sample_rows, z, y, core):
    groups = lax.axis_size("row")
    spread = jnp.broadcast_to(sample_rows, (groups, sample_rows.shape[0]))
    wanted = lax.all_to_all(spread, "row", 0, 0, tiled=True).reshape(-1)
    first_here, second_here = jnp.where(core == 0, y, z), jnp.where(core == 0, z, y)
    inner, outer = wanted % 1024, wanted // 1024
    outer_z, outer_y, outer_core = outer // 8, outer // 2 % 4, outer % 2
    first = jnp.where(core == 0, outer_y, outer_z)
    second = jnp.where(core == 0, outer_z, outer_y)
    both = (first & first_here) ^ (second & second_here)
    negative = (both ^ (both >> 1) ^ (outer_core & core)) & 1
    return (inner + 1024 * (first * 2 + outer_core) + 8192 * negative).astype(jnp.int32)


def shards(design, signs, sample_rows):
    owned = sample_rows.shape[0]
    myself = lax.axis_index("row")
    column = lax.axis_index("col")
    z, y, core = myself // 8, myself // 2 % 4, myself % 2
    first, second = jnp.where(core == 0, y, z), jnp.where(core == 0, z, y)
    where = jnp.stack([core, first, second, column]).astype(jnp.int32)
    total = owned * lax.axis_size("row")
    scale = float(np.float32(1.0) / np.sqrt(np.float32(total)))

    table = jnp.asarray(hadamard(256), jnp.bfloat16)
    pieces = local_transform(design, signs[None, :], table)
    own, theirs = pieces[:SIDE], list(pieces[SIDE:])
    sample_rows, _ = lax.optimization_barrier((sample_rows, own[0]))
    index = sample_index(sample_rows, z, y, core)
    index, theirs[0] = lax.optimization_barrier((index, theirs[0]))
    sources = [own[0]] + [hop(own[step], FIRST, step) for step in (1, 2, 3)]
    sources += [across(theirs[step], step) for step in range(SIDE)]

    gathered = []
    for chunk in range(2):
        picked = sampled_rows(where, index, sources, scale, chunk, owned)
        arrived = [hop(picked[step], SECOND, step) for step in (1, 2, 3)]
        sums = (picked[0] + arrived[0]) + (arrived[1] + arrived[2])
        mine = exchange(sums, FIRST)
        if gathered:
            mine, *_ = lax.optimization_barrier((mine, *gathered[0][1:4]))
        right, left = around(mine, 1), around(mine, 3)
        swapped, onward, back = mine, right, left
        if gathered:
            swapped, onward, back, *_ = lax.optimization_barrier((mine, right, left, *gathered[0][4:]))
        far_a, far_b = around(onward[: SIDE // 2], 1), around(back[SIDE // 2 :], 3)
        gathered.append((mine, to_sibling(swapped), right, left, far_a, far_b))

    sketch = sketch_rows(where, gathered[0][0], gathered[1][0], gathered[0][1], gathered[1][1])

    operands = gathered[0] + gathered[1]
    low, high = (0, 1), (2, 3)

    def blocks(*entries):
        return [(first, second) for first, seconds in entries for second in seconds]

    early_plan = [blocks((2, low), (1, low)), blocks((2, high), (3, high))]
    early = [gram_shares(where, operands, early_plan, (half,)) for half in range(2)]
    late = gram_shares(where, operands, [blocks((1, high)), blocks((3, low)), blocks((0, low), (0, high))], (0, 1))
    parts = []
    for half in range(2):
        to_one, to_three = early[half]
        rest_one, rest_three, here = late[half::2]
        from_one, from_three = hop(to_one, FIRST, 1), hop(to_three, FIRST, 3)
        last_one = hop(rest_one + from_three[:2], FIRST, 1)
        last_three = hop(rest_three + from_one[:2], FIRST, 3)
        sums = [here[0] + from_one[2] + last_three[0], here[1] + from_one[3] + last_three[1]]
        sums += [here[2] + from_three[2] + last_one[0], here[3] + from_three[3] + last_one[1]]
        arrived = [hop(sums[step], SECOND, step) for step in (1, 2, 3)]
        parts.append((sums[0] + arrived[0]) + (arrived[1] + arrived[2]))
    return (sketch, jnp.concatenate(parts, axis=1))


def solution(mesh):
    in_specs = (P("row", "col"), P("row"), P("row"))
    out_specs = (P("row", "col"), P("row", "col"))
    return jax.shard_map(shards, mesh=mesh, in_specs=in_specs, out_specs=out_specs, check_vma=False)
```
